32 devices in a mesh: dp: 16 (over z, y, x), mp: 2 (over core).
Axes of the slice: x: 2, y: 2, z: 4, core: 2. Of those that a mesh axis runs over, the one named last changes fastest.
Arguments:
- tokens: bfloat16 [16384, 768], P(('dp', 'mp')), may hold values from -6 to 6
- lengths: int32 [32, 8], P('dp'), may hold values from 1 to 256, 512 in all within a row
- cotangent: bfloat16 [16384, 768], P(('dp', 'mp')), may hold values from -6 to 6
- triple_weight: bfloat16 [768, 3, 768], P(None, None, 'mp'), may hold values from -0.21875 to 0.21875
- query_value_bias: bfloat16 [2, 768], P(None, 'mp'), may hold values from -3 to 3
- output_weight: bfloat16 [768, 768], P('mp'), may hold values from -0.875 to 0.875
- branch_bias: bfloat16 [2, 768], replicated, may hold values from -2 to 2
- expand_weight: bfloat16 [768, 3072], P(None, 'mp'), may hold values from -0.21875 to 0.21875
- expand_bias: bfloat16 [3072], P('mp'), may hold values from -2 to 2
- shrink_weight: bfloat16 [3072, 768], P('mp'), may hold values from -0.109375 to 0.109375
- adapter_down: float32 [2, 768, 64], replicated, may hold values from -0.21875 to 0.21875
- down_bias: float32 [2, 64], replicated, may hold values from -2 to 2
- adapter_up: float32 [2, 64, 768], replicated, may hold values from -0.75 to 0.75
- up_bias: float32 [2, 768], replicated, may hold values from -2 to 2
- norm_params: float32 [4, 768], replicated, may hold values from -1.2 to 1.4, as said below
- adapter_down_first: float32 [2, 768, 64], replicated, may hold values from -0.00390625 to 0.00390625
- adapter_down_second: float32 [2, 768, 64], replicated, may hold values from 2.4833122e-09 to 3.9732996e-08
- down_bias_first: float32 [2, 64], replicated, may hold values from -0.00390625 to 0.00390625
- down_bias_second: float32 [2, 64], replicated, may hold values from 2.4833122e-09 to 3.9732996e-08
- adapter_up_first: float32 [2, 64, 768], replicated, may hold values from -0.00390625 to 0.00390625
- adapter_up_second: float32 [2, 64, 768], replicated, may hold values from 2.4833122e-09 to 3.9732996e-08
- up_bias_first: float32 [2, 768], replicated, may hold values from -0.00390625 to 0.00390625
- up_bias_second: float32 [2, 768], replicated, may hold values from 7.449936e-10 to 5.959949e-09
- norm_params_first: float32 [4, 768], replicated, may hold values from -0.00390625 to 0.00390625
- norm_params_second: float32 [4, 768], replicated, may hold values from 2.4833122e-09 to 3.9732996e-08
- step: int32 [1], replicated, may hold values from 2 to 5
Outputs:
- output: float32 [16384, 768], P(('dp', 'mp'))
- input_grad: float32 [16384, 768], P(('dp', 'mp'))
- grad_norm: float32 [1], replicated
- adapter_down_new: float32 [2, 768, 64], replicated
- adapter_down_first_new: float32 [2, 768, 64], replicated
- adapter_down_second_new: float32 [2, 768, 64], replicated
- down_bias_new: float32 [2, 64], replicated
- down_bias_first_new: float32 [2, 64], replicated
- down_bias_second_new: float32 [2, 64], replicated
- adapter_up_new: float32 [2, 64, 768], replicated
- adapter_up_first_new: float32 [2, 64, 768], replicated
- adapter_up_second_new: float32 [2, 64, 768], replicated
- up_bias_new: float32 [2, 768], replicated
- up_bias_first_new: float32 [2, 768], replicated
- up_bias_second_new: float32 [2, 768], replicated
- norm_params_new: float32 [4, 768], replicated
- norm_params_first_new: float32 [4, 768], replicated
- norm_params_second_new: float32 [4, 768], replicated
The draws below stay inside these ranges and needn't reach their ends.
Inputs may be any that keep to these rules, and one draw needn't show every extreme that they name: Each packed row of 512 tokens holds 8 pairs back to back whose lengths sum to 512; some pair in the batch has exactly 256 tokens. `norm_params`: rows 0 and 2 are gains, rows 1 and 3 shifts.
All inputs are finite; a program needn't handle non-finite values.
Results may differ from the reference program's by a relative error of at most 0.018.
Values may be sent and summed in bfloat16 or wider, within the bound.
A program may use at most 128 MiB of HBM per device.

```python
import math
import jax
import jax.numpy as jnp
import numpy as np
from jax import lax

D = 768
FF = 3072
RANK = 64
PACK = 512
SLOTS = 8
MOST = 256
HEAD_DIM = 64
ROWS = 32
TOKENS = 16384
PARAMS = 201344


def draw_norm_params(key, part):
    gain_key, shift_key = jax.random.split(jax.random.fold_in(key, 11))
    gains = jax.random.uniform(gain_key, (2, D), jnp.float32, 0.6, 1.4)
    shifts = jnp.clip(0.3 * jax.random.normal(shift_key, (2, D), jnp.float32), -1.2, 1.2)
    return jnp.stack([gains[0], shifts[0], gains[1], shifts[1]], 0)


def shard_levels(key, extent, shards, smallest, high):
    level = 1.0
    for position, parts in shards:
        steps = jax.random.uniform(jax.random.fold_in(jax.random.fold_in(key, 6), position), (parts,), jnp.float32, smallest / len(shards), high / len(shards))
        level = level * jnp.repeat(jnp.exp(steps), extent[position] // parts).reshape((-1,) + (1,) * (len(extent) - 1 - position))
    return level


def profile(amount, total, reach, skew):
    loads = [(1 << 20) // math.isqrt(grade ** skew) + 1 for grade in range(2, amount + 1)]
    rest, counts = total - reach - (amount - 1), [1] * (amount - 1)
    while rest > 0:
        movable = [i for i in range(amount - 1) if counts[i] < reach]
        whole, budget = sum([loads[i] for i in movable]), rest
        for i in movable:
            more = min(reach - counts[i], max(1, budget * loads[i] // whole), rest)
            counts[i] = counts[i] + more
            rest = rest - more
    return np.array([reach] + counts)


def ragged_sizes(rng, count, total, limit, slope):
    if count == 2:
        one = jax.random.randint(rng, (), max(1, total - limit), min(limit, total - 1) + 1)
        return jnp.stack([one, total - one])
    sizes = jnp.asarray(profile(count, total, limit, slope), jnp.int32)
    pairs = (count - 1) // 2
    giver, sink = sizes[1:1 + 2 * pairs:2], sizes[2:2 + 2 * pairs:2]
    slack = jnp.minimum(giver - 1, limit - sink)
    moved = jax.random.randint(jax.random.fold_in(rng, 1), (pairs,), 0, 1 << 20) % (slack + 1)
    sizes = sizes.at[1:1 + 2 * pairs:2].set(giver - moved).at[2:2 + 2 * pairs:2].set(sink + moved)
    return sizes[jax.random.permutation(jax.random.fold_in(rng, 2), count)]


def bell_draw(key, extent, deviation, limit, pieces=(), kind=jnp.bfloat16):
    values = jax.random.normal(key, extent, jnp.float32) * deviation
    if len(pieces) > 0:
        values = shard_levels(key, extent, pieces, -0.22, 0.18) * values
    return jnp.clip(values, min=-limit, max=limit).astype(kind)


def setup_inputs(seed: int = 0) -> dict:
    splits = jax.random.split(jax.random.key(seed), 27)
    return {
        "tokens": bell_draw(splits[0], (TOKENS, D), 1.0, 6.0, ((0, 32),)),
        "lengths": jax.vmap(lambda own: ragged_sizes(own, SLOTS, PACK, MOST, 2))(jax.random.split(splits[1], ROWS)).reshape((ROWS, SLOTS)).astype(jnp.int32),
        "cotangent": bell_draw(splits[2], (TOKENS, D), 1.0, 6.0, ((0, 32),)),
        "triple_weight": bell_draw(splits[3], (D, 3, D), D ** -0.5, 0.21875, ((2, 2),)),
        "query_value_bias": bell_draw(splits[4], (2, D), 0.5, 3.0, ((1, 2),)),
        "output_weight": bell_draw(splits[5], (D, D), (D // 16) ** -0.5, 0.875, ((0, 2),)),
        "branch_bias": bell_draw(splits[6], (2, D), 0.3, 2.0),
        "expand_weight": bell_draw(splits[7], (D, FF), D ** -0.5, 0.21875, ((1, 2),)),
        "expand_bias": bell_draw(splits[8], (FF,), 0.3, 2.0, ((0, 2),)),
        "shrink_weight": bell_draw(splits[9], (FF, D), FF ** -0.5, 0.109375, ((0, 2),)),
        "adapter_down": bell_draw(splits[10], (2, D, RANK), D ** -0.5, 0.21875, (), jnp.float32),
        "down_bias": bell_draw(splits[11], (2, RANK), 0.3, 2.0, (), jnp.float32),
        "adapter_up": bell_draw(splits[12], (2, RANK, D), RANK ** -0.5, 0.75, (), jnp.float32),
        "up_bias": bell_draw(splits[13], (2, D), 0.3, 2.0, (), jnp.float32),
        "norm_params": draw_norm_params(jax.random.fold_in(splits[26], 71), 0),
        "adapter_down_first": bell_draw(splits[15], (2, D, RANK), (0.11 / PARAMS ** 0.5), 0.00390625, (), jnp.float32),
        "adapter_down_second": jnp.clip(jnp.exp(jax.random.uniform(splits[16], (2, D, RANK), jnp.float32, math.log(2.483312222523182e-09), math.log(3.973299556037091e-08))), 2.483312222523182e-09, 3.973299556037091e-08),
        "down_bias_first": bell_draw(splits[17], (2, RANK), (0.11 / PARAMS ** 0.5), 0.00390625, (), jnp.float32),
        "down_bias_second": jnp.clip(jnp.exp(jax.random.uniform(splits[18], (2, RANK), jnp.float32, math.log(2.483312222523182e-09), math.log(3.973299556037091e-08))), 2.483312222523182e-09, 3.973299556037091e-08),
        "adapter_up_first": bell_draw(splits[19], (2, RANK, D), (0.11 / PARAMS ** 0.5), 0.00390625, (), jnp.float32),
        "adapter_up_second": jnp.clip(jnp.exp(jax.random.uniform(splits[20], (2, RANK, D), jnp.float32, math.log(2.483312222523182e-09), math.log(3.973299556037091e-08))), 2.483312222523182e-09, 3.973299556037091e-08),
        "up_bias_first": bell_draw(splits[21], (2, D), (0.11 / PARAMS ** 0.5), 0.00390625, (), jnp.float32),
        "up_bias_second": jnp.clip(jnp.exp(jax.random.uniform(splits[22], (2, D), jnp.float32, math.log(7.449936223480336e-10), math.log(5.9599489787842685e-09))), 7.449936223480336e-10, 5.9599489787842685e-09),
        "norm_params_first": bell_draw(splits[23], (4, D), (0.11 / PARAMS ** 0.5), 0.00390625, (), jnp.float32),
        "norm_params_second": jnp.clip(jnp.exp(jax.random.uniform(splits[24], (4, D), jnp.float32, math.log(2.483312222523182e-09), math.log(3.973299556037091e-08))), 2.483312222523182e-09, 3.973299556037091e-08),
        "step": jax.random.randint(splits[25], (1,), 2, 6).astype(jnp.int32),
    }


NEGATIVE = -1e+30
PRECISE = lax.Precision.HIGHEST

@jax.custom_vjp
def low(v):
    return lax.optimization_barrier(v.astype(jnp.bfloat16)).astype(jnp.float32)

@jax.custom_vjp
def low_back(v):
    return v

def low_keep(v):
    return (low(v), None)

def low_pass(kept, grad):
    return (grad,)

def back_keep(v):
    return (v, None)

def back_low(kept, grad):
    return (low(grad),)
low.defvjp(low_keep, low_pass)
low_back.defvjp(back_keep, back_low)

def matmul(left, right):
    return jnp.dot(left, right, precision=PRECISE)

def layer_norm(value, gain, shift):
    center = value - lax.optimization_barrier(jnp.mean(value, axis=-1, keepdims=True))
    scale = lax.rsqrt(lax.optimization_barrier(jnp.mean(center * center, axis=-1, keepdims=True)) + 1e-12)
    return center * scale * gain + shift

def adapter(branch, index, train):
    down_w, down_b, up_w, up_b, unused = train
    inner = low_back(matmul(low(branch), low(down_w[index])) + down_b[index])
    activity = low(jax.nn.gelu(inner, approximate=False))
    return branch + low_back(matmul(activity, low(up_w[index])) + up_b[index])

def row_layer(train, frozen, packed, marks):
    triple_w, pair_b, output_w, branch_b, expand_w, expand_b, shrink_w = frozen
    norms = train[4]
    count = packed.shape[0]
    heads = D // HEAD_DIM
    triple_b = jnp.stack([pair_b[0], jnp.zeros((D,), jnp.float32), pair_b[1]], 0)
    mixed = jnp.einsum('td,dcn->tcn', packed, triple_w, precision=PRECISE) + triple_b
    mixed = low_back(low(mixed))
    query_rows = mixed[:, 0].reshape(count, heads, HEAD_DIM)
    key_rows = mixed[:, 1].reshape(count, heads, HEAD_DIM)
    value_rows = mixed[:, 2].reshape(count, heads, HEAD_DIM)
    scores = jnp.einsum('qhd,khd->hqk', query_rows, key_rows, precision=PRECISE) * HEAD_DIM ** (-0.5)
    allowed = marks[:, None] == marks[None, :]
    scores = low_back(jnp.where(allowed[None], scores, NEGATIVE))
    probs = low(jax.nn.softmax(scores, axis=-1))
    attended = jnp.einsum('hqk,khd->qhd', probs, value_rows, precision=PRECISE).reshape(count, D)
    attended = low_back(low(attended))
    branch = low_back(matmul(attended, output_w) + branch_b[0])
    first = layer_norm(packed + adapter(branch, 0, train), norms[0], norms[1])
    before = low_back(matmul(low(first), expand_w) + expand_b)
    hidden = low(jax.nn.gelu(before, approximate=False))
    second = low_back(matmul(hidden, shrink_w) + branch_b[1])
    return layer_norm(first + adapter(second, 1, train), norms[2], norms[3])

def adam_step(weight, grad, first, second, rate, decay, clip, fix_one, fix_two):
    clipped = grad * clip
    first_new = 0.9 * first + 0.1 * clipped
    second_new = 0.999 * second + 0.001 * clipped * clipped
    update = first_new / fix_one / (jnp.sqrt(second_new / fix_two) + 1e-08) + decay * weight
    return (weight - rate * update, first_new, second_new)

def reference(tokens, lengths, cotangent, triple_weight, query_value_bias, output_weight, branch_bias, expand_weight, expand_bias, shrink_weight, adapter_down, down_bias, adapter_up, up_bias, norm_params, adapter_down_first, adapter_down_second, down_bias_first, down_bias_second, adapter_up_first, adapter_up_second, up_bias_first, up_bias_second, norm_params_first, norm_params_second, step):
    ends = jnp.cumsum(lengths, axis=-1).astype(jnp.int32)
    places = jnp.arange(PACK, dtype=jnp.int32)
    pair_ids = lax.optimization_barrier(jnp.sum((places[None, :, None] >= ends[:, None, :-1]).astype(jnp.int32), axis=-1))
    frozen = tuple((w.astype(jnp.float32) for w in (triple_weight, query_value_bias, output_weight, branch_bias, expand_weight, expand_bias, shrink_weight)))
    train = (adapter_down, down_bias, adapter_up, up_bias, norm_params)
    rows = tokens.astype(jnp.float32).reshape(ROWS, PACK, D)

    def forward(params, inputs):
        one = jax.checkpoint(lambda item: row_layer(params, frozen, item[0], item[1]))
        return lax.map(one, (inputs, pair_ids))
    output, pull = jax.vjp(forward, train, rows)
    grads, input_grad = pull(cotangent.astype(jnp.float32).reshape(ROWS, PACK, D))
    total = jnp.float32(0.0)
    for grad in grads:
        total = total + jnp.sum(grad * grad)
    grad_norm = jnp.sqrt(total)
    clip = jnp.minimum(1.0, 1.0 / (grad_norm + 1e-06))
    count = step[0].astype(jnp.float32)
    fix_one = 1.0 - jnp.power(0.9, count)
    fix_two = 1.0 - jnp.power(0.999, count)
    rates = ((0.03, 0.01), (0.1, 0.0), (0.1, 0.01), (0.1, 0.0), (0.2, 0.0))
    firsts = (adapter_down_first, down_bias_first, adapter_up_first, up_bias_first, norm_params_first)
    seconds = (adapter_down_second, down_bias_second, adapter_up_second, up_bias_second, norm_params_second)
    results = []
    for index in range(5):
        results.extend(adam_step(train[index], grads[index], firsts[index], seconds[index], rates[index][0], rates[index][1], clip, fix_one, fix_two))
    return (output.reshape(TOKENS, D), input_grad.reshape(TOKENS, D), grad_norm.reshape(1), results[0], results[1], results[2], results[3], results[4], results[5], results[6], results[7], results[8], results[9], results[10], results[11], results[12], results[13], results[14])
```

```python
import functools

import jax
import jax.numpy as jnp
from jax import lax
from jax.experimental import pallas as pl
from jax.experimental.pallas import tpu as pltpu
from jax.sharding import PartitionSpec as P

HEAD_DIM = 64
SLOTS = 8
EPSILON = 1e-12
CLIP_LIMIT = 1.0
LOG2E = 1.4426950408889634
HALF_ROOT = 0.7071067811865476
DENSITY = 0.3989422804014327
NEGATIVE = -1e30
RATES = ((0.03, 0.01), (0.1, 0.0), (0.1, 0.01), (0.1, 0.0), (0.2, 0.0))
PART = 80
MESH = pl.DeviceIdType.MESH
BF = jnp.bfloat16
F32 = jnp.float32


def nn(a, b):
    return lax.dot_general(a, b, (((1,), (0,)), ((), ())), preferred_element_type=F32)


def nt(a, b):
    return lax.dot_general(a, b, (((1,), (1,)), ((), ())), preferred_element_type=F32)


def tn(a, b):
    return lax.dot_general(a, b, (((0,), (0,)), ((), ())), preferred_element_type=F32)


def at(start, size, step=None):
    if isinstance(start, int):
        return pl.ds(start, size)
    return pl.ds(pl.multiple_of(start, step or size), size)


def gelu_parts(value):
    mass = 0.5 + 0.5 * lax.erf(value * HALF_ROOT)
    slope = mass + value * (jnp.exp2(value * value * (-0.5 * LOG2E)) * DENSITY)
    return value * mass, slope


def fold_rows(value):
    rows, width = value.shape
    return jnp.sum(value.reshape(rows // 8, 8, width), axis=0)


def layer_kernel(
    sizes,
    lengths,
    qv_bias,
    branch_bias,
    expand_bias,
    down_bias,
    up_bias,
    norms,
    tokens_hbm,
    cot_hbm,
    triple_hbm,
    out_w_hbm,
    expand_hbm,
    shrink_hbm,
    down_hbm,
    up_hbm,
    output_hbm,
    input_grad_hbm,
    sums_hbm,
    xs,
    cots,
    w3,
    wo,
    we,
    ws,
    down_f,
    up_f,
    down_l,
    up_l,
    bias_own,
    bias_far,
    kt,
    vt,
    q_t,
    k_t,
    v_t,
    hot,
    qa,
    ex,
    fac,
    o_t,
    att,
    br_l0,
    br_l1,
    act0,
    act1,
    gd0,
    gd1,
    gl,
    inl,
    normed,
    scale_s,
    first_f,
    first_l,
    hid,
    slope,
    ssg,
    sgl,
    tmp,
    tmp2,
    dqkv,
    outs,
    grads,
    acc,
    c_recv,
    rs_buf,
    rs_recv,
    ag_buf,
    ag_far,
    load_sem,
    far_send,
    far_recv,
    core_send,
    core_recv,
    ring_send,
    ring_recv,
    store_sem,
):
    tok, width, half, ff_half, n_dp, piece = sizes
    ff = 2 * ff_half
    wide = 3 * half
    heads_half = half // HEAD_DIM
    pairs_half = heads_half // 2
    dp = lax.axis_index("dp")
    mp = lax.axis_index("mp")
    mate = (dp, 1 - mp)

    def load(src, dst, index):
        copy = pltpu.make_async_copy(src, dst, load_sem.at[index])
        copy.start()
        return copy

    load_x = load(tokens_hbm, xs, 0)
    load_w3 = [
        load(triple_hbm.at[c], w3.at[:, at(c * half, half)], 1 + c) for c in range(3)
    ]
    load_down = load(down_hbm, down_f, 4)
    load_up = load(up_hbm, up_f, 5)
    load_wo = load(out_w_hbm, wo.at[at(0, half), :], 6)
    load_we = load(expand_hbm, we.at[:, at(0, ff_half)], 7)
    load_ws = load(shrink_hbm, ws.at[at(0, ff_half), :], 8)
    load_cot = load(cot_hbm, cots, 9)

    barrier = pltpu.get_barrier_semaphore()
    pl.semaphore_signal(barrier, inc=1, device_id=mate, device_id_type=MESH)

    def greet(step, carry):
        peer = lax.rem(dp + step, n_dp)
        pl.semaphore_signal(barrier, inc=1, device_id=(peer, mp), device_id_type=MESH)
        return carry

    lax.fori_loop(1, n_dp, greet, 0)

    bias_own[...] = jnp.zeros_like(bias_own)
    bias_own[0:2, 0:half] = qv_bias[...].astype(F32)
    bias_own[2:3, :] = expand_bias[...].astype(F32)

    ends = []
    total = jnp.int32(0)
    for slot in range(SLOTS - 1):
        total = total + jnp.where(mp == 0, lengths[0, slot], lengths[1, slot])
        ends.append(total)

    def marks(shape, axis):
        place = lax.broadcasted_iota(jnp.int32, shape, axis)
        found = jnp.zeros(shape, jnp.int32)
        for end in ends:
            found = found + (place >= end).astype(jnp.int32)
        return found

    hot[...] = jnp.where(
        marks((tok, 128), 0) == lax.broadcasted_iota(jnp.int32, (tok, 128), 1), 1.0, 0.0
    ).astype(BF)
    shut = jnp.where(
        marks((128, tok), 1) == lax.broadcasted_iota(jnp.int32, (128, tok), 0), 0.0, NEGATIVE
    ).astype(BF)
    for slot in range(4):
        qa[at(slot * 256, 128), :] = jnp.zeros((128, tok), BF)
        qa[at(slot * 256 + 128, 128), :] = shut
    grads[...] = jnp.zeros_like(grads)
    acc[...] = jnp.zeros_like(acc)
    rs_buf[...] = jnp.zeros_like(rs_buf)

    pl.semaphore_wait(barrier, n_dp)

    def push(src, dst, index):
        copy = pltpu.make_async_remote_copy(
            src_ref=src,
            dst_ref=dst,
            send_sem=far_send.at[index],
            recv_sem=far_recv.at[index],
            device_id=mate,
            device_id_type=MESH,
        )
        copy.start()
        return copy

    far_bias = push(bias_own, bias_far, 0)
    far_w3 = [
        push(triple_hbm.at[c], w3.at[:, at(wide + c * half, half)], 1 + c) for c in range(3)
    ]

    load_x.wait()
    for copy in load_w3:
        copy.wait()

    def project(side, bias):
        base = side * wide
        rows = at(side * half, half)
        for c in range(3):
            mixed = nn(xs[...], w3[:, at(base + c * half, half)])
            if c == 0:
                mixed = mixed + bias[0:1, 0:half]
            if c == 2:
                mixed = mixed + bias[1:2, 0:half]
            low = mixed.astype(BF)
            if c == 0:
                q_t[rows, :] = (low.astype(F32) * (HEAD_DIM ** -0.5)).astype(BF).T
            if c == 1:
                kt[:, rows] = low
                k_t[rows, :] = low.T
            if c == 2:
                vt[:, rows] = low
                v_t[rows, :] = low.T

    span = tok // 2
    ones = jnp.ones((16, tok), BF)

    def attend(pair, carry):
        for j in range(2):
            qa[at(j * 256 + j * 64, 64), :] = q_t[at(pair * 128 + j * 64, 64), :]
        cols = at(pair * 128, 128)
        keys = jnp.concatenate([kt[:, cols], hot[...]], axis=1)
        results = []
        for j in range(2):
            head = pair * 2 + j
            rows = at(pair * 128 + j * 64, 64)
            peaks = []
            for kh in range(2):
                tops = []
                for c in range(2):
                    s = nn(
                        keys[kh * span : (kh + 1) * span], qa[at(j * 256, 256), at(c * span, span)]
                    )
                    top = jnp.max(s, axis=0, keepdims=True) * LOG2E
                    ex[head, at(kh * span, span), at(c * span, span)] = jnp.exp2(
                        s * LOG2E - top
                    ).astype(BF)
                    tops.append(top)
                peaks.append(jnp.concatenate(tops, axis=1))
            values = jnp.concatenate([v_t[rows, :], ones], axis=0)
            parts = [
                nn(values[:, kh * span : (kh + 1) * span], ex[head, at(kh * span, span), :])
                for kh in range(2)
            ]
            peak = jnp.maximum(peaks[0], peaks[1])
            weights = [jnp.exp2(p - peak) for p in peaks]
            inverse = 1.0 / (parts[0][64:65] * weights[0] + parts[1][64:65] * weights[1])
            weights = [w * inverse for w in weights]
            fac[head, 0:1, :] = weights[0]
            fac[head, 1:2, :] = weights[1]
            result = (parts[0][:64] * weights[0] + parts[1][:64] * weights[1]).astype(BF)
            o_t[rows, :] = result
            results.append(result)
        att[:, cols] = jnp.concatenate(results, axis=0).T
        return carry

    project(0, bias_own)
    far_wo = push(out_w_hbm, wo.at[at(half, half), :], 4)
    far_we = push(expand_hbm, we.at[:, at(ff_half, ff_half)], 5)
    lax.fori_loop(0, pairs_half, attend, 0)
    far_ws = push(shrink_hbm, ws.at[at(ff_half, ff_half), :], 6)
    far_bias.wait()
    for copy in far_w3:
        copy.wait()
    project(1, bias_far)
    lax.fori_loop(pairs_half, 2 * pairs_half, attend, 0)

    load_down.wait()
    load_up.wait()
    down_l[...] = down_f[...].astype(BF)
    up_l[...] = up_f[...].astype(BF)
    load_wo.wait()
    far_wo.wait()

    chunk = 256
    sub = 32
    bias_rows = branch_bias[...].astype(F32)

    def normalize(v):
        center = v - jnp.mean(v, axis=-1, keepdims=True)
        scale = lax.rsqrt(jnp.mean(center * center, axis=-1, keepdims=True) + EPSILON)
        return center * scale, scale

    def adapter_in(index, base, br_l, act, gd):
        rows = at(base, chunk)
        inner = nt(br_l[rows, :], down_l[index]) + down_bias[index : index + 1, :]
        value, grade = gelu_parts(inner)
        act[rows, :] = value.astype(BF)
        gd[rows, :] = grade
        tmp2[rows, :] = nn(act[rows, :], up_l[index])

    for base in range(0, tok, chunk):
        tmp[at(base, chunk), :] = nn(att[at(base, chunk), :], wo[...])
        for r in range(base, base + chunk, sub):
            rows = at(r, sub)
            value = tmp[rows, :] + bias_rows[0:1]
            tmp[rows, :] = value
            br_l0[rows, :] = value.astype(BF)
        adapter_in(0, base, br_l0, act0, gd0)
        for r in range(base, base + chunk, sub):
            rows = at(r, sub)
            value = xs[rows, :].astype(F32) + tmp[rows, :] + tmp2[rows, :] + up_bias[0:1, :]
            unit, scale = normalize(value)
            normed[rows, :] = unit
            scale_s[rows, :] = scale
            first = unit * norms[0:1, :] + norms[1:2, :]
            first_f[rows, :] = first
            first_l[rows, :] = first.astype(BF)

    load_we.wait()

    def expand(side, bias):
        def body(j, carry):
            cols = at(side * ff_half + j * 256, 256)
            shift = bias[2:3, at(j * 256, 256)]
            for r in range(0, tok, 256):
                before = nn(first_l[at(r, 256), :], we[:, cols]) + shift
                value, grade = gelu_parts(before)
                hid[at(r, 256), cols] = value.astype(BF)
                slope[at(r, 256), cols] = grade.astype(BF)
            return carry

        lax.fori_loop(0, ff_half // 256, body, 0)

    expand(0, bias_own)
    far_we.wait()
    expand(1, bias_far)
    load_ws.wait()
    load_cot.wait()
    far_ws.wait()

    def norm_back(grad, unit, scale, gain, slot):
        acc[at(slot * 8, 8), :] += fold_rows(grad * unit)
        acc[at(slot * 8 + 8, 8), :] += fold_rows(grad)
        inner = grad * gain
        back = scale * (
            inner
            - jnp.mean(inner, axis=-1, keepdims=True)
            - unit * jnp.mean(inner * unit, axis=-1, keepdims=True)
        )
        low = back.astype(BF)
        acc[at(slot * 8 + 16, 8), :] += fold_rows(low.astype(F32))
        return back, low

    def adapter_out(index, base, gd, target):
        rows = at(base, chunk)
        inner = (nt(gl[rows, :], up_l[index]) * gd[rows, :]).astype(BF)
        inl[rows, :] = inner
        tmp2[rows, :] = nn(inner, down_l[index])
        for r in range(base, base + chunk, sub):
            part = at(r, sub)
            target[part, :] = (ssg[part, :] + tmp2[part, :]).astype(BF)

    def collect(index, act, br_l, slot):
        grads[index, 0, 0:64, :] = tn(inl[...], br_l[...])
        grads[index, 1, 0:64, :] = tn(act[...], gl[...])
        for n, place in ((0, (0, 64)), (1, (0, 65)), (2, (1, 64))):
            line = jnp.sum(acc[at((slot + n) * 8, 8), :], axis=0, keepdims=True)
            grads[index, place[0], place[1] : place[1] + 1, :] = line
        grads[index, 1, 65:66, 0:64] = jnp.sum(inl[...].astype(F32), axis=0, keepdims=True)

    def core_copy(b):
        return pltpu.make_async_remote_copy(
            src_ref=grads.at[b, 1 - mp],
            dst_ref=c_recv.at[b],
            send_sem=core_send.at[2 * b],
            recv_sem=core_recv.at[2 * b],
            device_id=mate,
            device_id_type=MESH,
        )

    def ring_copy(b, stage, step):
        peer = lax.rem(dp + step, n_dp)
        if stage == 0:
            src, dst = rs_buf.at[b, peer], rs_recv.at[b, step - 1]
        else:
            src, dst = ag_buf.at[b, dp], ag_buf.at[b, dp]
        return pltpu.make_async_remote_copy(
            src_ref=src,
            dst_ref=dst,
            send_sem=ring_send.at[2 * b + stage],
            recv_sem=ring_recv.at[2 * b + stage],
            device_id=(peer, mp),
            device_id_type=MESH,
        )

    def ring_start(b, stage):
        def body(step, carry):
            ring_copy(b, stage, step).start()
            return carry

        lax.fori_loop(1, n_dp, body, 0)

    def ring_wait(b, stage):
        block = rs_recv.at[b]
        pltpu.make_async_copy(block, block, ring_send.at[2 * b + stage]).wait()
        pltpu.make_async_copy(block, block, ring_recv.at[2 * b + stage]).wait()

    def last_copy(b):
        return pltpu.make_async_remote_copy(
            src_ref=ag_buf.at[b],
            dst_ref=ag_far.at[b],
            send_sem=core_send.at[2 * b + 1],
            recv_sem=core_recv.at[2 * b + 1],
            device_id=mate,
            device_id_type=MESH,
        )

    def reduce_one(b):
        core_copy(b).start()

    def reduce_two(b):
        core_copy(b).wait()
        mine = (grads[b, mp] + c_recv[b]).astype(BF)
        blocks = jnp.concatenate(
            [mine[:, c * 128 : (c + 1) * 128] for c in range(width // 128)], axis=0
        )
        flat = blocks.shape[0]
        spare = n_dp * piece - flat
        if spare:
            blocks = jnp.concatenate([blocks, jnp.zeros((spare, 128), BF)], axis=0)
        rs_buf[b] = blocks.reshape(n_dp, piece, 128)
        ring_start(b, 0)

    def reduce_three(b):
        ring_wait(b, 0)

        def add(step, total):
            return total + rs_recv[b, step].astype(F32)

        total = lax.fori_loop(0, n_dp - 1, add, rs_buf[b, dp].astype(F32))
        ag_buf[b, dp] = total.astype(BF)
        ring_start(b, 1)

    def reduce_four(b):
        ring_wait(b, 1)
        last_copy(b).start()

    def reduce_five(b):
        last_copy(b).wait()

    for base in range(0, tok, chunk):
        tmp[at(base, chunk), :] = nn(hid[at(base, chunk), :], ws[...])
        for r in range(base, base + chunk, sub):
            rows = at(r, sub)
            value = tmp[rows, :] + bias_rows[1:2]
            tmp[rows, :] = value
            br_l1[rows, :] = value.astype(BF)
        adapter_in(1, base, br_l1, act1, gd1)
        for r in range(base, base + chunk, sub):
            rows = at(r, sub)
            value = first_f[rows, :] + tmp[rows, :] + tmp2[rows, :] + up_bias[1:2, :]
            unit, scale = normalize(value)
            outs[rows, :] = unit * norms[2:3, :] + norms[3:4, :]
            back, low = norm_back(cots[rows, :].astype(F32), unit, scale, norms[2:3, :], 0)
            ssg[rows, :] = back
            gl[rows, :] = low
        adapter_out(1, base, gd1, sgl)

    store_out = pltpu.make_async_copy(outs, output_hbm, store_sem.at[0])
    store_out.start()
    collect(1, act1, br_l1, 0)
    reduce_one(1)

    def unshrink(j, carry):
        cols = at(j * 256, 256)
        for r in range(0, tok, 256):
            grad = nt(sgl[at(r, 256), :], ws[cols, :])
            hid[at(r, 256), cols] = (grad * slope[at(r, 256), cols].astype(F32)).astype(BF)
        return carry

    lax.fori_loop(0, ff // 256, unshrink, 0)
    reduce_two(1)

    for base in range(0, tok, chunk):
        tmp[at(base, chunk), :] = nt(hid[at(base, chunk), :], we[...])
        for r in range(base, base + chunk, sub):
            rows = at(r, sub)
            back, low = norm_back(
                ssg[rows, :] + tmp[rows, :], normed[rows, :], scale_s[rows, :], norms[0:1, :], 3
            )
            ssg[rows, :] = back
            gl[rows, :] = low
        adapter_out(0, base, gd0, sgl)
    collect(0, act0, br_l0, 3)
    reduce_one(0)
    reduce_three(1)

    d_t = v_t
    for base in range(0, width, 256):
        hid[0:256, at(base * 2, 512)] = nt(wo[at(base, 256), :], sgl[...]).astype(BF)
    reduce_two(0)

    def attend_back(pair, carry):
        cols = at(pair * 128, 128)
        values = vt[:, cols]
        got = [[], [], []]
        for j in range(2):
            head = pair * 2 + j
            rows = at(pair * 128 + j * 64, 64)
            grad = grad_of(pair, j)
            dot = jnp.sum(grad * o_t[rows, :].astype(F32), axis=0, keepdims=True)
            score_grads = []
            value_grads = []
            for kh in range(2):
                weight = fac[head, kh : kh + 1, :]
                scaled = (grad * weight).astype(BF)
                pieces = [scaled, jnp.zeros((64, tok), BF)]
                spread = jnp.concatenate(pieces if j == 0 else pieces[::-1], axis=0)
                back = nn(values[kh * span : (kh + 1) * span], spread)
                exps = ex[head, at(kh * span, span), :]
                score_grads.append((exps.astype(F32) * (back - dot * weight)).astype(BF))
                value_grads.append(nt(scaled, exps))
            scores = jnp.concatenate(score_grads, axis=0)
            got[0].append((nn(k_t[rows, :], scores) * (HEAD_DIM ** -0.5)).astype(BF))
            got[1].append(nt(q_t[rows, :], scores).astype(BF))
            got[2].append(jnp.concatenate(value_grads, axis=1).astype(BF))
        side = lax.div(pair, pairs_half)
        offset = side * wide + lax.rem(pair, pairs_half) * 128
        for c in range(3):
            dqkv[:, at(offset + c * half, 128)] = jnp.concatenate(got[c], axis=0).T
        return carry

    def grad_of(pair, j):
        block = lax.div(pair, 2)
        row = lax.rem(pair, 2) * 128 + j * 64
        return hid[at(row, 64), at(block * 512, 512)].astype(F32)

    lax.fori_loop(0, pairs_half, attend_back, 0)
    reduce_three(0)
    reduce_four(1)
    lax.fori_loop(pairs_half, 2 * pairs_half, attend_back, 0)
    reduce_four(0)
    store_out.wait()
    for base in range(0, tok, chunk):
        rows = at(base, chunk)
        outs[rows, :] = ssg[rows, :] + nt(dqkv[rows, :], w3[...])
    store_in = pltpu.make_async_copy(outs, input_grad_hbm, store_sem.at[0])
    store_in.start()
    reduce_five(1)
    reduce_five(0)
    ends_ = []
    for b in range(2):
        for index, (src, side) in enumerate(((ag_buf, mp), (ag_far, 1 - mp))):
            copy = pltpu.make_async_copy(
                src.at[b], sums_hbm.at[b, side], store_sem.at[1 + 2 * b + index]
            )
            copy.start()
            ends_.append(copy)
    for copy in ends_:
        copy.wait()
    store_in.wait()


def update_kernel(
    blocks,
    step,
    output_src,
    input_grad_src,
    sums,
    *refs,
):
    params, rest = refs[:15], refs[15:]
    output, input_grad, norm_out = rest[:3]
    news = rest[3:18]
    sem = rest[18]
    copies = [
        pltpu.make_async_copy(output_src, output, sem.at[0]),
        pltpu.make_async_copy(input_grad_src, input_grad, sem.at[1]),
    ]
    for copy in copies:
        copy.start()
    squares = jnp.zeros((8, 128), F32)
    for b in range(2):
        for side in range(2):
            part = sums[b, side].astype(F32)
            squares = squares + fold_rows(part * part)
    squares = jnp.sum(jnp.sum(squares, axis=0, keepdims=True), axis=1, keepdims=True)
    grad_norm = jnp.sqrt(squares)
    norm_out[...] = grad_norm
    clip = jnp.minimum(1.0, CLIP_LIMIT / (grad_norm + 1e-06))
    count = jnp.full((1, 1), step[0], jnp.int32).astype(F32)
    fix_one = 1.0 - jnp.exp2(count * jnp.log2(jnp.full((1, 1), 0.9, F32)))
    fix_two = 1.0 - jnp.exp2(count * jnp.log2(jnp.full((1, 1), 0.999, F32)))
    over_one = 1.0 / fix_one
    over_two = 1.0 / fix_two

    def update(index, where, grad):
        weight, first, second = (params[3 * index + n][where] for n in range(3))
        rate, decay = RATES[index]
        clipped = grad * clip
        first_new = 0.9 * first + 0.1 * clipped
        second_new = 0.999 * second + 0.001 * clipped * clipped
        move = first_new * over_one / (jnp.sqrt(second_new * over_two) + 1e-08)
        if decay:
            move = move + decay * weight
        news[3 * index][where] = weight - rate * move
        news[3 * index + 1][where] = first_new
        news[3 * index + 2][where] = second_new

    for b in range(2):
        lines = []
        for side in range(2):
            tops = []
            for c in range(blocks):
                block = sums[b, side, pl.ds(c * PART, PART), :].astype(F32)
                update(
                    2 * side, (b, slice(None), slice(c * 128, (c + 1) * 128)), block[0:64]
                )
                tops.append(block[64:72])
            lines.append(jnp.concatenate(tops, axis=1))
        update(4, (slice(2 * b, 2 * b + 2), slice(None)), lines[0][0:2])
        update(3, (slice(b, b + 1), slice(None)), lines[1][0:1])
        update(1, (slice(b, b + 1), slice(None)), lines[1][1:2, 0:64])
    for copy in copies:
        copy.wait()


def per_device(
    n_dp,
    tokens,
    lengths,
    cotangent,
    triple_weight,
    query_value_bias,
    output_weight,
    branch_bias,
    expand_weight,
    expand_bias,
    shrink_weight,
    adapter_down,
    down_bias,
    adapter_up,
    up_bias,
    norm_params,
    adapter_down_first,
    adapter_down_second,
    down_bias_first,
    down_bias_second,
    adapter_up_first,
    adapter_up_second,
    up_bias_first,
    up_bias_second,
    norm_params_first,
    norm_params_second,
    step,
):
    tok, width = tokens.shape
    half = triple_weight.shape[2]
    ff_half = expand_weight.shape[1]
    ff = 2 * ff_half
    heads = 2 * half // HEAD_DIM
    blocks = width // 128
    piece = -(-(PART * blocks) // (16 * n_dp)) * 16
    sizes = (tok, width, half, ff_half, n_dp, piece)
    flip = lambda v: jnp.swapaxes(v, 1, 2)
    vmem = pl.BlockSpec(memory_space=pltpu.VMEM)
    smem = pl.BlockSpec(memory_space=pltpu.SMEM)
    any_ = pl.BlockSpec(memory_space=pl.ANY)
    V = pltpu.VMEM
    D = pltpu.SemaphoreType.DMA
    down_flip = flip(adapter_down)
    output, input_grad, sums = pl.pallas_call(
        functools.partial(layer_kernel, sizes),
        out_shape=(
            jax.ShapeDtypeStruct((tok, width), F32),
            jax.ShapeDtypeStruct((tok, width), F32),
            jax.ShapeDtypeStruct((2, 2, n_dp, piece, 128), BF),
        ),
        in_specs=[smem] + [vmem] * 6 + [any_] * 8,
        out_specs=(any_, any_, any_),
        scratch_shapes=[
            V((tok, width), BF),
            V((tok, width), BF),
            V((width, 6 * half), BF),
            V((2 * half, width), BF),
            V((width, ff), BF),
            V((ff, width), BF),
            V((2, 64, width), F32),
            V((2, 64, width), F32),
            V((2, 64, width), BF),
            V((2, 64, width), BF),
            V((8, ff_half), F32),
            V((8, ff_half), F32),
            V((tok, width), BF),
            V((tok, width), BF),
            V((width, tok), BF),
            V((width, tok), BF),
            V((width, tok), BF),
            V((tok, 128), BF),
            V((4 * 256, tok), BF),
            V((heads, tok, tok), BF),
            V((heads, 8, tok), F32),
            V((width, tok), BF),
            V((tok, width), BF),
            V((tok, width), BF),
            V((tok, width), BF),
            V((tok, 64), BF),
            V((tok, 64), BF),
            V((tok, 64), F32),
            V((tok, 64), F32),
            V((tok, width), BF),
            V((tok, 64), BF),
            V((tok, width), F32),
            V((tok, 1), F32),
            V((tok, width), F32),
            V((tok, width), BF),
            V((tok, ff), BF),
            V((tok, ff), BF),
            V((tok, width), F32),
            V((tok, width), BF),
            V((tok, width), F32),
            V((tok, width), F32),
            V((tok, 6 * half), BF),
            V((tok, width), F32),
            V((2, 2, PART, width), F32),
            V((48, width), F32),
            V((2, PART, width), F32),
            V((2, n_dp, piece, 128), BF),
            V((2, n_dp - 1, piece, 128), BF),
            V((2, n_dp, piece, 128), BF),
            V((2, n_dp, piece, 128), BF),
            D((10,)),
            D((7,)),
            D((7,)),
            D((4,)),
            D((4,)),
            D((4,)),
            D((4,)),
            D((5,)),
        ],
        compiler_params=pltpu.CompilerParams(
            collective_id=0, has_side_effects=True, vmem_limit_bytes=62 * 2**20
        ),
    )(
        lengths,
        query_value_bias,
        branch_bias,
        expand_bias.reshape(1, ff_half),
        down_bias,
        up_bias,
        norm_params,
        tokens,
        cotangent,
        jnp.transpose(triple_weight, (1, 0, 2)),
        output_weight,
        expand_weight,
        shrink_weight,
        down_flip,
        adapter_up,
    )
    sums = sums.reshape(2, 2, n_dp * piece, 128)
    params = (
        down_flip,
        flip(adapter_down_first),
        flip(adapter_down_second),
        down_bias,
        down_bias_first,
        down_bias_second,
        adapter_up,
        adapter_up_first,
        adapter_up_second,
        up_bias,
        up_bias_first,
        up_bias_second,
        norm_params,
        norm_params_first,
        norm_params_second,
    )
    shapes = [jax.ShapeDtypeStruct(p.shape, F32) for p in params]
    results = pl.pallas_call(
        functools.partial(update_kernel, blocks),
        out_shape=(
            jax.ShapeDtypeStruct((tok, width), F32),
            jax.ShapeDtypeStruct((tok, width), F32),
            jax.ShapeDtypeStruct((1, 1), F32),
            *shapes,
        ),
        in_specs=[smem, any_, any_] + [vmem] * 16,
        out_specs=(any_, any_) + (vmem,) * 16,
        scratch_shapes=[D((2,))],
        compiler_params=pltpu.CompilerParams(vmem_limit_bytes=32 * 2**20),
    )(step, output, input_grad, sums, *params)
    news = list(results[3:])
    for index in range(3):
        news[index] = flip(news[index])
    return (results[0], results[1], results[2].reshape(1), *news)


def solution(mesh):
    split = P(("dp", "mp"), None)
    in_specs = (
        split,
        P("dp", None),
        split,
        P(None, None, "mp"),
        P(None, "mp"),
        P("mp", None),
        P(),
        P(None, "mp"),
        P("mp"),
        P("mp", None),
    ) + (P(),) * 16
    out_specs = (split, split) + (P(),) * 16
    return jax.shard_map(
        functools.partial(per_device, mesh.shape["dp"]),
        mesh=mesh,
        in_specs=in_specs,
        out_specs=out_specs,
        check_vma=False,
    )
```

```python
import functools
import types

import jax
import jax.numpy as jnp
from jax import lax
from jax.experimental import pallas as pl
from jax.experimental.pallas import tpu as pltpu
from jax.sharding import PartitionSpec as P

HEAD_DIM = 64
SLOTS = 8
EPSILON = 1e-12
CLIP_LIMIT = 1.0
LOG2E = 1.4426950408889634
HALF_ROOT = 0.7071067811865476
DENSITY = 0.3989422804014327
NEGATIVE = -1e30
RATES = ((0.03, 0.01), (0.1, 0.0), (0.1, 0.01), (0.1, 0.0), (0.2, 0.0))
PART = 80
MESH = pl.DeviceIdType.MESH
BF = jnp.bfloat16
F32 = jnp.float32


def nn(a, b):
    return lax.dot_general(a, b, (((1,), (0,)), ((), ())), preferred_element_type=F32)


def nt(a, b):
    return lax.dot_general(a, b, (((1,), (1,)), ((), ())), preferred_element_type=F32)


def tn(a, b):
    return lax.dot_general(a, b, (((0,), (0,)), ((), ())), preferred_element_type=F32)


def at(start, size, step=None):
    if isinstance(start, int):
        return pl.ds(start, size)
    return pl.ds(pl.multiple_of(start, step or size), size)


def gelu_parts(value):
    mass = 0.5 + 0.5 * lax.erf(value * HALF_ROOT)
    slope = mass + value * (jnp.exp2(value * value * (-0.5 * LOG2E)) * DENSITY)
    return value * mass, slope


def fold_rows(value):
    rows, width = value.shape
    return jnp.sum(value.reshape(rows // 8, 8, width), axis=0)


SCRATCH = (
    ("xs", lambda z: ((z.tok, z.width), BF)),
    ("cots", lambda z: ((z.tok, z.width), BF)),
    ("w3", lambda z: ((z.width, 6 * z.half), BF)),
    ("wo", lambda z: ((2 * z.half, z.width), BF)),
    ("we", lambda z: ((z.width, z.ff), BF)),
    ("ws", lambda z: ((z.ff, z.width), BF)),
    ("down_l", lambda z: ((2, 64, z.width), BF)),
    ("up_l", lambda z: ((2, 64, z.width), BF)),
    ("bias_own", lambda z: ((8, z.ff_half), F32)),
    ("bias_far", lambda z: ((8, z.ff_half), F32)),
    ("keys", lambda z: ((z.tok, z.width), BF)),
    ("values", lambda z: ((z.tok, z.width), BF)),
    ("q_t", lambda z: ((z.width, z.tok), BF)),
    ("k_t", lambda z: ((z.width, z.tok), BF)),
    ("v_t", lambda z: ((z.width, z.tok), BF)),
    ("hot", lambda z: ((z.tok, 128), BF)),
    ("qa", lambda z: ((4 * 256, z.tok), BF)),
    ("ex", lambda z: ((z.heads, z.tok, z.tok), BF)),
    ("fac", lambda z: ((z.heads, 8, z.tok), F32)),
    ("o_t", lambda z: ((z.width, z.tok), BF)),
    ("att", lambda z: ((z.tok, z.width), BF)),
    ("br_l", lambda z: ((2, z.tok, z.width), BF)),
    ("act", lambda z: ((2, z.tok, 128), BF)),
    ("gd", lambda z: ((2, z.tok, 64), F32)),
    ("inl", lambda z: ((z.tok, 64), BF)),
    ("normed", lambda z: ((z.tok, z.width), F32)),
    ("scale_s", lambda z: ((z.tok, 1), F32)),
    ("first_f", lambda z: ((z.tok, z.width), F32)),
    ("first_l", lambda z: ((z.tok, z.width), BF)),
    ("hid", lambda z: ((z.tok, z.ff), BF)),
    ("slope", lambda z: ((z.tok, z.ff), BF)),
    ("tmp", lambda z: ((z.tok, z.width), F32)),
    ("grads", lambda z: ((2, 2, PART, z.width), F32)),
    ("acc", lambda z: ((48, z.width), F32)),
    ("c_recv", lambda z: ((2, PART, z.width), F32)),
    ("rs_buf", lambda z: ((2, z.n_dp, z.piece, 128), BF)),
    ("rs_recv", lambda z: ((2, z.n_dp - 1, z.piece, 128), BF)),
    ("ag_buf", lambda z: ((2, z.n_dp, z.piece, 128), BF)),
    ("ag_far", lambda z: ((2, z.n_dp, z.piece, 128), BF)),
)
SEMAPHORES = (
    ("load_sem", 25),
    ("meet", 0),
    ("far_send", 7),
    ("far_recv", 7),
    ("core_send", 4),
    ("core_recv", 4),
    ("ring_send", 4),
    ("ring_recv", 4),
)
INPUTS = (
    ("lengths", "s"),
    ("qv_bias", "v"),
    ("branch_bias", "v"),
    ("expand_bias", "v"),
    ("down_bias", "v"),
    ("up_bias", "v"),
    ("norms", "v"),
    ("tokens", "h"),
    ("cot", "h"),
    ("triple", "h"),
    ("out_w", "h"),
    ("expand", "h"),
    ("shrink", "h"),
    *((f"param{index}", "h") for index in range(15)),
)
CHUNK = 256
SUB = 32


def weave(*works):
    queues = [[list(work), 0] for work in works]
    most = max(len(queue[0]) for queue in queues)
    for tick in range(most):
        for queue in queues:
            units, done = queue
            goal = -(-len(units) * (tick + 1) // most)
            for unit in units[done:goal]:
                unit()
            queue[1] = max(done, goal)


def normalize(v):
    center = v - jnp.mean(v, axis=-1, keepdims=True)
    scale = lax.rsqrt(jnp.mean(center * center, axis=-1, keepdims=True) + EPSILON)
    return center * scale, scale


def set_masks(z, r, ends):
    def marks(shape, axis):
        place = lax.broadcasted_iota(jnp.int32, shape, axis)
        found = jnp.zeros(shape, jnp.int32)
        for end in ends:
            found = found + (place >= end).astype(jnp.int32)
        return found

    tok = z.tok
    r.hot[...] = jnp.where(
        marks((tok, 128), 0) == lax.broadcasted_iota(jnp.int32, (tok, 128), 1), 1.0, 0.0
    ).astype(BF)
    shut = jnp.where(
        marks((128, tok), 1) == lax.broadcasted_iota(jnp.int32, (128, tok), 0), 0.0, NEGATIVE
    ).astype(BF)
    for slot in range(4):
        r.qa[at(slot * 256, 128), :] = jnp.zeros((128, tok), BF)
        r.qa[at(slot * 256 + 128, 128), :] = shut


def project(z, r, side):
    bias = (r.bias_own, r.bias_far)[side]
    base = side * 3 * z.half
    rows = at(side * z.half, z.half)
    for c in range(3):
        mixed = nn(r.xs[...], r.w3[:, at(base + c * z.half, z.half)])
        if c == 0:
            mixed = mixed + bias[0:1, 0 : z.half]
        if c == 2:
            mixed = mixed + bias[1:2, 0 : z.half]
        low = mixed.astype(BF)
        if c == 0:
            r.q_t[rows, :] = (low.astype(F32) * (HEAD_DIM ** -0.5)).astype(BF).T
        if c == 1:
            r.keys[:, rows] = low
            r.k_t[rows, :] = low.T
        if c == 2:
            r.values[:, rows] = low
            r.v_t[rows, :] = low.T


def attend(z, r, side):
    span = z.tok // 2
    first = side * z.half // HEAD_DIM
    count = z.half // HEAD_DIM
    ones = jnp.ones((16, z.tok), BF)
    kept = {}

    def scores(head):
        slot = head % 4
        r.qa[at(slot * 256 + (head % 2) * 64, 64), :] = r.q_t[at(head * 64, 64), :]
        keys = jnp.concatenate([r.keys[:, at(head // 2 * 128, 128)], r.hot[...]], axis=1)
        peaks = []
        for kh in range(2):
            tops = []
            for c in range(2):
                s = nn(keys[kh * span : (kh + 1) * span], r.qa[at(slot * 256, 256), at(c * span, span)])
                top = jnp.max(s, axis=0, keepdims=True) * LOG2E
                r.ex[head, at(kh * span, span), at(c * span, span)] = jnp.exp2(
                    s * LOG2E - top
                ).astype(BF)
                tops.append(top)
            peaks.append(jnp.concatenate(tops, axis=1))
        kept[head] = peaks

    def gather(head):
        rows = at(head * 64, 64)
        values = jnp.concatenate([r.v_t[rows, :], ones], axis=0)
        parts = [
            nn(values[:, kh * span : (kh + 1) * span], r.ex[head, at(kh * span, span), :])
            for kh in range(2)
        ]
        peaks = kept.pop(head)
        peak = jnp.maximum(peaks[0], peaks[1])
        weights = [jnp.exp2(p - peak) for p in peaks]
        inverse = 1.0 / (parts[0][64:65] * weights[0] + parts[1][64:65] * weights[1])
        weights = [w * inverse for w in weights]
        r.fac[head, 0:1, :] = weights[0]
        r.fac[head, 1:2, :] = weights[1]
        r.o_t[rows, :] = (parts[0][:64] * weights[0] + parts[1][:64] * weights[1]).astype(BF)
        if head % 2:
            cols = at(head // 2 * 128, 128)
            r.att[:, cols] = r.o_t[cols, :].T

    for head in range(first, first + count):
        scores(head)
        if head > first:
            gather(head - 1)
    gather(first + count - 1)


def big_dot(z, base, left, right, form, finish):
    rows = at(base, CHUNK)
    for n in range(0, z.width, 256):

        def unit(n=n):
            cols = at(n, 256)
            weights = right[:, cols] if form is nn else right[cols, :]
            finish(rows, cols, form(left[rows, :], weights))

        yield unit


def branch_out(z, r, index, base, left, right, before):
    def finish(rows, cols, product):
        value = product + r.branch_bias[index : index + 1, cols].astype(F32)
        r.br_l[index, rows, cols] = value.astype(BF)
        r.tmp[rows, cols] = value + before[rows, cols].astype(F32)

    return big_dot(z, base, left, right, nn, finish)


def adapt(z, r, index, base):
    def inner():
        rows = at(base, CHUNK)
        value, grade = gelu_parts(
            nt(r.br_l[index, rows, :], r.down_l[index]) + r.down_bias[index : index + 1, :]
        )
        low = value.astype(BF)
        r.act[index, rows, 0:64] = low
        r.gd[index, rows, :] = grade
        for n in range(0, z.width, 256):
            cols = at(n, 256)
            r.tmp[rows, cols] += nn(low, r.up_l[index, :, cols]) + r.up_bias[index : index + 1, cols]

    yield inner


def first_norm(z, r, base):
    yield from adapt(z, r, 0, base)
    for row in range(base, base + CHUNK, SUB):

        def unit(row=row):
            rows = at(row, SUB)
            normed, scale = normalize(r.tmp[rows, :])
            r.normed[rows, :] = normed
            r.scale_s[rows, :] = scale
            first = normed * r.norms[0:1, :] + r.norms[1:2, :]
            r.first_f[rows, :] = first
            r.first_l[rows, :] = first.astype(BF)

        yield unit


def expand(z, r, side, base):
    bias = (r.bias_own, r.bias_far)[side]
    rows = at(base, CHUNK)
    for j in range(0, z.ff_half, 256):

        def unit(j=j):
            cols = at(side * z.ff_half + j, 256)
            before = nn(r.first_l[rows, :], r.we[:, cols]) + bias[2:3, at(j, 256)]
            value, grade = gelu_parts(before)
            r.hid[rows, cols] = value.astype(BF)
            r.slope[rows, cols] = grade.astype(BF)

        yield unit


def unshrink(z, r, base):
    rows = at(base, CHUNK)
    for j in range(0, z.ff, 256):

        def unit(j=j):
            cols = at(j, 256)
            grad = nt(r.sgl[rows, :], r.ws[cols, :])
            r.hid[rows, cols] = (grad * r.slope[rows, cols].astype(F32)).astype(BF)

        yield unit


def norm_back(sums, grad, unit, scale, gain):
    for place, part in enumerate((fold_rows(grad * unit), fold_rows(grad))):
        sums[place] = part if sums[place] is None else sums[place] + part
    inner = grad * gain
    back = scale * (
        inner
        - jnp.mean(inner, axis=-1, keepdims=True)
        - unit * jnp.mean(inner * unit, axis=-1, keepdims=True)
    )
    return back, back.astype(BF)


def adapter_out(z, r, index, base, sums):
    def inner():
        rows = at(base, CHUNK)
        low = (nt(r.gl[rows, :], r.up_l[index]) * r.gd[index, rows, :]).astype(BF)
        r.inl[rows, :] = low
        for n in range(0, z.width, 256):
            cols = at(n, 256)
            r.sgl[rows, cols] = (r.ssg[rows, cols] + nn(low, r.down_l[index, :, cols])).astype(BF)
        for place in range(2):
            lines = at((2 * index + place) * 8, 8)
            r.acc[lines, :] = sums[place] if base == 0 else r.acc[lines, :] + sums[place]

    yield inner


def second_norm(z, r, base):
    yield from adapt(z, r, 1, base)
    sums = [None, None]
    for row in range(base, base + CHUNK, SUB):

        def unit(row=row):
            rows = at(row, SUB)
            normed, scale = normalize(r.tmp[rows, :])
            r.output[rows, :] = normed * r.norms[2:3, :] + r.norms[3:4, :]
            back, low = norm_back(
                sums, r.cots[rows, :].astype(F32), normed, scale, r.norms[2:3, :]
            )
            r.ssg[rows, :] = back
            r.gl[rows, :] = low

        yield unit
    yield from adapter_out(z, r, 1, base, sums)


def first_out(z, r, base):
    def finish(rows, cols, product):
        r.tmp[rows, cols] = product + r.ssg[rows, cols]

    return big_dot(z, base, r.hid, r.we, nt, finish)


def first_back(z, r, base):
    sums = [None, None]
    for row in range(base, base + CHUNK, SUB):

        def unit(row=row):
            rows = at(row, SUB)
            back, low = norm_back(
                sums, r.tmp[rows, :], r.normed[rows, :], r.scale_s[rows, :], r.norms[0:1, :]
            )
            r.ssg[rows, :] = back
            r.gl[rows, :] = low

        yield unit
    yield from adapter_out(z, r, 0, base, sums)


def collect(z, r, index):
    def down():
        r.grads[index, 0, 0:64, :] = tn(r.inl[...], r.br_l[index])

    def up():
        r.grads[index, 1, 0:72, :] = tn(r.act[index], r.gl[...])[0:72]

    def lines():
        for place in range(2):
            line = jnp.sum(r.acc[at((2 * index + place) * 8, 8), :], axis=0, keepdims=True)
            r.grads[index, 0, 64 + place : 65 + place, :] = line
        r.grads[index, 1, 65:66, 0:64] = jnp.sum(r.inl[...].astype(F32), axis=0, keepdims=True)

    yield down
    yield up
    yield lines


def branch_back(z, r, base):
    for row in range(0, z.width, 256):

        def unit(row=row):
            rows = at(row, 256)
            r.dat[rows, at(base, CHUNK)] = nt(r.wo[rows, :], r.sgl[at(base, CHUNK), :]).astype(BF)

        yield unit


def attend_back(z, r, pair):
    span = z.tok // 2
    cols = at(pair * 128, 128)
    values = r.values[:, cols]
    got = [[], [], []]
    for j in range(2):
        head = pair * 2 + j
        rows = at(pair * 128 + j * 64, 64)
        grad = r.dat[rows, :].astype(F32)
        dot = jnp.sum(grad * r.o_t[rows, :].astype(F32), axis=0, keepdims=True)
        score_grads = []
        value_grads = []
        for kh in range(2):
            weight = r.fac[head, kh : kh + 1, :]
            scaled = (grad * weight).astype(BF)
            pieces = [scaled, jnp.zeros((64, z.tok), BF)]
            spread = jnp.concatenate(pieces if j == 0 else pieces[::-1], axis=0)
            back = nn(values[kh * span : (kh + 1) * span], spread)
            exps = r.ex[head, at(kh * span, span), :]
            score_grads.append((exps.astype(F32) * (back - dot * weight)).astype(BF))
            value_grads.append(nt(scaled, exps))
        scores = jnp.concatenate(score_grads, axis=0)
        got[0].append((nn(r.k_t[rows, :], scores) * (HEAD_DIM ** -0.5)).astype(BF))
        got[1].append(nt(r.q_t[rows, :], scores).astype(BF))
        got[2].append(jnp.concatenate(value_grads, axis=1).astype(BF))
    pairs_half = z.half // 128
    side = lax.div(pair, pairs_half)
    offset = side * 3 * z.half + lax.rem(pair, pairs_half) * 128
    for c in range(3):
        r.dqkv[:, at(offset + c * z.half, 128)] = jnp.concatenate(got[c], axis=0).T


def input_back(z, r, base):
    rows = at(base, CHUNK)
    r.input_grad[rows, :] = r.ssg[rows, :] + nt(r.dqkv[rows, 0 : 6 * z.half], r.w3[...])


def share(r):
    r.dqkv, r.dat, r.sgl, r.gl, r.ssg = r.slope, r.v_t, r.first_l, r.att, r.first_f


def layer_kernel(z, *refs):
    names = [name for name, _ in INPUTS] + ["output", "input_grad", "sums"]
    names += [f"held{index}" for index in range(15)]
    names += [name for name, _ in SCRATCH] + [name for name, _ in SEMAPHORES]
    r = types.SimpleNamespace(**dict(zip(names, refs, strict=True)))
    share(r)
    tok, width, half, ff_half, n_dp, piece = z.tok, z.width, z.half, z.ff_half, z.n_dp, z.piece
    wide = 3 * half
    dp = lax.axis_index("dp")
    mp = lax.axis_index("mp")
    mate = (dp, 1 - mp)

    def load(src, dst, index):
        copy = pltpu.make_async_copy(src, dst, r.load_sem.at[index])
        copy.start()
        return copy

    load_x = load(r.tokens, r.xs, 0)
    load_w3 = [load(r.triple.at[c], r.w3.at[:, at(c * half, half)], 1 + c) for c in range(3)]

    barrier = pltpu.get_barrier_semaphore()
    ready, go = r.meet.at[0], r.meet.at[1]

    @pl.when(mp == 0)
    def call():
        pl.semaphore_signal(barrier, inc=1, device_id=mate, device_id_type=MESH)

    load_down = load(r.param0, r.held0, 4)
    load_up = load(r.param6, r.held6, 5)
    load_wo = load(r.out_w, r.wo.at[at(0, half), :], 6)
    load_we = load(r.expand, r.we.at[:, at(0, ff_half)], 7)
    load_ws = load(r.shrink, r.ws.at[at(0, ff_half), :], 8)
    load_cot = load(r.cot, r.cots, 9)

    r.bias_own[...] = jnp.zeros_like(r.bias_own)
    r.bias_own[0:2, 0:half] = r.qv_bias[...].astype(F32)
    r.bias_own[2:3, :] = r.expand_bias[...].astype(F32).reshape(1, ff_half)

    ends = []
    total = jnp.int32(0)
    for slot in range(SLOTS - 1):
        total = total + jnp.where(mp == 0, r.lengths[0, slot], r.lengths[1, slot])
        ends.append(total)

    @pl.when(mp == 1)
    def answer():
        pl.semaphore_wait(barrier, 1)
        pl.semaphore_signal(ready, inc=1, device_id=mate, device_id_type=MESH)

    @pl.when(mp == 0)
    def hear():
        pl.semaphore_wait(ready, 1)

        def greet(step, carry):
            peer = lax.rem(dp + step, n_dp)
            pl.semaphore_signal(barrier, inc=1, device_id=(peer, mp), device_id_type=MESH)
            return carry

        lax.fori_loop(1, n_dp, greet, 0)

    def gather_all():
        @pl.when(mp == 0)
        def first_core():
            pl.semaphore_wait(barrier, n_dp - 1)
            pl.semaphore_signal(go, inc=1, device_id=mate, device_id_type=MESH)

        @pl.when(mp == 1)
        def second_core():
            pl.semaphore_wait(go, 1)

    def push(src, dst, index):
        copy = pltpu.make_async_remote_copy(
            src_ref=src,
            dst_ref=dst,
            send_sem=r.far_send.at[index],
            recv_sem=r.far_recv.at[index],
            device_id=mate,
            device_id_type=MESH,
        )
        copy.start()
        return copy

    far_bias = push(r.bias_own, r.bias_far, 0)
    far_w3 = [
        push(r.triple.at[c], r.w3.at[:, at(wide + c * half, half)], 1 + c) for c in range(3)
    ]
    set_masks(z, r, ends)
    r.grads[...] = jnp.zeros_like(r.grads)
    marker = lax.broadcasted_iota(jnp.int32, (tok, 128), 1) == 64
    for index in range(2):
        r.act[index] = jnp.where(marker, 1.0, 0.0).astype(BF)
    load_x.wait()
    for copy in load_w3:
        copy.wait()
    project(z, r, 0)
    far_wo = push(r.out_w, r.wo.at[at(half, half), :], 4)
    far_we = push(r.expand, r.we.at[:, at(ff_half, ff_half)], 5)
    attend(z, r, 0)
    far_ws = push(r.shrink, r.ws.at[at(ff_half, ff_half), :], 6)
    far_bias.wait()
    for copy in far_w3:
        copy.wait()
    project(z, r, 1)
    attend(z, r, 1)

    load_down.wait()
    load_up.wait()
    r.down_l[...] = r.held0[...].astype(BF)
    r.up_l[...] = r.held6[...].astype(BF)
    held = [
        load(getattr(r, f"param{index}"), getattr(r, f"held{index}"), 10 + index)
        for index in range(15)
        if index not in (0, 6)
    ]
    load_wo.wait()
    far_wo.wait()
    load_we.wait()

    def core_copy(b):
        return pltpu.make_async_remote_copy(
            src_ref=r.grads.at[b, 1 - mp],
            dst_ref=r.c_recv.at[b],
            send_sem=r.core_send.at[2 * b],
            recv_sem=r.core_recv.at[2 * b],
            device_id=mate,
            device_id_type=MESH,
        )

    def ring_start(b, stage):
        def body(step, carry):
            peer = lax.rem(dp + step, n_dp)
            if stage == 0:
                src, dst = r.rs_buf.at[b, peer], r.rs_recv.at[b, step - 1]
            else:
                src, dst = r.ag_buf.at[b, dp], r.ag_buf.at[b, dp]
            pltpu.make_async_remote_copy(
                src_ref=src,
                dst_ref=dst,
                send_sem=r.ring_send.at[2 * b + stage],
                recv_sem=r.ring_recv.at[2 * b + stage],
                device_id=(peer, mp),
                device_id_type=MESH,
            ).start()
            return carry

        lax.fori_loop(1, n_dp, body, 0)

    def ring_wait(b, stage):
        block = r.rs_recv.at[b]
        pltpu.make_async_copy(block, block, r.ring_send.at[2 * b + stage]).wait()
        pltpu.make_async_copy(block, block, r.ring_recv.at[2 * b + stage]).wait()

    def last_copy(b):
        return pltpu.make_async_remote_copy(
            src_ref=r.ag_buf.at[b],
            dst_ref=r.ag_far.at[b],
            send_sem=r.core_send.at[2 * b + 1],
            recv_sem=r.core_recv.at[2 * b + 1],
            device_id=mate,
            device_id_type=MESH,
        )

    def reduce_one(b):
        core_copy(b).start()

    def reduce_two(b):
        core_copy(b).wait()
        mine = (r.grads[b, mp] + r.c_recv[b]).astype(BF)
        blocks = jnp.concatenate(
            [mine[:, c * 128 : (c + 1) * 128] for c in range(width // 128)], axis=0
        )
        spare = n_dp * piece - blocks.shape[0]
        if spare:
            blocks = jnp.concatenate([blocks, jnp.zeros((spare, 128), BF)], axis=0)
        r.rs_buf[b] = blocks.reshape(n_dp, piece, 128)
        ring_start(b, 0)

    def reduce_three(b):
        ring_wait(b, 0)

        def add(step, total):
            return total + r.rs_recv[b, step].astype(F32)

        total = lax.fori_loop(0, n_dp - 1, add, r.rs_buf[b, dp].astype(F32))
        r.ag_buf[b, dp] = total.astype(BF)
        ring_start(b, 1)

    def reduce_four(b):
        ring_wait(b, 1)
        last_copy(b).start()

    def reduce_five(b):
        last_copy(b).wait()

    late = CHUNK
    att, hid = r.att, r.hid
    weave(branch_out(z, r, 0, 0, att, r.wo, r.xs))
    weave(branch_out(z, r, 0, late, att, r.wo, r.xs), first_norm(z, r, 0))
    weave(expand(z, r, 0, 0), first_norm(z, r, late))
    weave(expand(z, r, 0, late))
    far_we.wait()
    weave(expand(z, r, 1, 0))
    weave(expand(z, r, 1, late))
    gather_all()
    load_ws.wait()
    load_cot.wait()
    far_ws.wait()
    weave(branch_out(z, r, 1, 0, hid, r.ws, r.first_f))
    weave(branch_out(z, r, 1, late, hid, r.ws, r.first_f), second_norm(z, r, 0))
    weave(unshrink(z, r, 0), second_norm(z, r, late))
    weave(unshrink(z, r, late), collect(z, r, 1))
    reduce_one(1)
    weave(first_out(z, r, 0))
    reduce_two(1)
    weave(first_out(z, r, late), first_back(z, r, 0))
    weave(branch_back(z, r, 0), first_back(z, r, late))
    weave(collect(z, r, 0), branch_back(z, r, late))
    reduce_one(0)

    def back(pair, carry):
        attend_back(z, r, pair)
        return carry

    pairs = width // 128
    lax.fori_loop(0, 1, back, 0)
    reduce_two(0)
    reduce_three(1)
    lax.fori_loop(1, pairs, back, 0)
    reduce_three(0)
    reduce_four(1)
    for base in range(0, tok, CHUNK):
        input_back(z, r, base)
    for copy in held:
        copy.wait()
    reduce_five(1)
    reduce_four(0)
    for b in range(2):
        r.sums[b, mp] = r.ag_buf[b]
    r.sums[1, 1 - mp] = r.ag_far[1]
    reduce_five(0)
    r.sums[0, 1 - mp] = r.ag_far[0]


def update_kernel(blocks, step, output_src, input_grad_src, sums, *refs):
    params, rest = refs[:15], refs[15:]
    output, input_grad, norm_out = rest[:3]
    targets, news, sem = rest[3:18], rest[18:33], rest[33]
    stores = []

    def store(src, dst):
        copy = pltpu.make_async_copy(src, dst, sem.at[len(stores)])
        copy.start()
        stores.append(copy)

    store(output_src, output)
    store(input_grad_src, input_grad)
    squares = jnp.zeros((8, 128), F32)
    for b in range(2):
        for side in range(2):
            part = sums[b, side].astype(F32)
            squares = squares + fold_rows(part * part)
    squares = jnp.sum(jnp.sum(squares, axis=0, keepdims=True), axis=1, keepdims=True)
    grad_norm = jnp.sqrt(squares)
    norm_out[...] = grad_norm
    clip = jnp.minimum(1.0, CLIP_LIMIT / (grad_norm + 1e-06))
    count = jnp.full((1, 1), step[0], jnp.int32).astype(F32)
    fix_one = 1.0 - jnp.exp2(count * jnp.log2(jnp.full((1, 1), 0.9, F32)))
    fix_two = 1.0 - jnp.exp2(count * jnp.log2(jnp.full((1, 1), 0.999, F32)))
    over_one = 1.0 / fix_one
    over_two = 1.0 / fix_two

    def update(index, where, grad):
        weight, first, second = (params[3 * index + n][where] for n in range(3))
        rate, decay = RATES[index]
        clipped = grad * clip
        first_new = 0.9 * first + 0.1 * clipped
        second_new = 0.999 * second + 0.001 * clipped * clipped
        move = first_new * over_one / (jnp.sqrt(second_new * over_two) + 1e-08)
        if decay:
            move = move + decay * weight
        news[3 * index][where] = weight - rate * move
        news[3 * index + 1][where] = first_new
        news[3 * index + 2][where] = second_new

    for b in range(2):
        lines = []
        for side in range(2):
            tops = []
            for c in range(blocks):
                block = sums[b, side, pl.ds(c * PART, PART), :].astype(F32)
                update(
                    2 * side, (b, slice(None), slice(c * 128, (c + 1) * 128)), block[0:64]
                )
                tops.append(block[64:72])
            lines.append(jnp.concatenate(tops, axis=1))
        update(4, (slice(2 * b, 2 * b + 2), slice(None)), lines[0][0:2])
        update(3, (slice(b, b + 1), slice(None)), lines[1][0:1])
        update(1, (slice(b, b + 1), slice(None)), lines[1][1:2, 0:64])
    for index in range(15):
        store(news[index], targets[index])
    for copy in stores:
        copy.wait()


def per_device(
    n_dp,
    tokens,
    lengths,
    cotangent,
    triple_weight,
    query_value_bias,
    output_weight,
    branch_bias,
    expand_weight,
    expand_bias,
    shrink_weight,
    adapter_down,
    down_bias,
    adapter_up,
    up_bias,
    norm_params,
    adapter_down_first,
    adapter_down_second,
    down_bias_first,
    down_bias_second,
    adapter_up_first,
    adapter_up_second,
    up_bias_first,
    up_bias_second,
    norm_params_first,
    norm_params_second,
    step,
):
    tok, width = tokens.shape
    half = triple_weight.shape[2]
    ff_half = expand_weight.shape[1]
    ff = 2 * ff_half
    heads = 2 * half // HEAD_DIM
    blocks = width // 128
    piece = -(-(PART * blocks) // (16 * n_dp)) * 16
    z = types.SimpleNamespace(
        tok=tok,
        width=width,
        half=half,
        ff_half=ff_half,
        ff=ff,
        heads=heads,
        n_dp=n_dp,
        piece=piece,
    )
    flip = lambda v: jnp.swapaxes(v, 1, 2)
    spaces = {
        "s": pl.BlockSpec(memory_space=pltpu.SMEM),
        "v": pl.BlockSpec(memory_space=pltpu.VMEM),
        "h": pl.BlockSpec(memory_space=pltpu.HBM),
    }
    vmem, smem, hbm = spaces["v"], spaces["s"], spaces["h"]
    params = (
        flip(adapter_down),
        flip(adapter_down_first),
        flip(adapter_down_second),
        down_bias,
        down_bias_first,
        down_bias_second,
        adapter_up,
        adapter_up_first,
        adapter_up_second,
        up_bias,
        up_bias_first,
        up_bias_second,
        norm_params,
        norm_params_first,
        norm_params_second,
    )
    operands = (
        lengths,
        query_value_bias,
        branch_bias,
        expand_bias,
        down_bias,
        up_bias,
        norm_params,
        tokens,
        cotangent,
        jnp.transpose(triple_weight, (1, 0, 2)),
        output_weight,
        expand_weight,
        shrink_weight,
        *params,
    )
    output, input_grad, sums, *held = pl.pallas_call(
        functools.partial(layer_kernel, z),
        out_shape=(
            pltpu.VMEM((tok, width), F32),
            pltpu.VMEM((tok, width), F32),
            pltpu.VMEM((2, 2, n_dp, piece, 128), BF),
            *(pltpu.VMEM(p.shape, F32) for p in params),
        ),
        in_specs=[spaces[space] for _, space in INPUTS],
        out_specs=(vmem,) * 18,
        scratch_shapes=[pltpu.VMEM(*make(z)) for _, make in SCRATCH]
        + [
            pltpu.SemaphoreType.DMA((count,)) if count else pltpu.SemaphoreType.REGULAR((2,))
            for _, count in SEMAPHORES
        ],
        compiler_params=pltpu.CompilerParams(
            collective_id=0, has_side_effects=True, vmem_limit_bytes=56 * 2**20
        ),
    )(*operands)
    sums = sums.reshape(2, 2, n_dp * piece, 128)
    results = pl.pallas_call(
        functools.partial(update_kernel, blocks),
        out_shape=(
            jax.ShapeDtypeStruct((tok, width), F32),
            jax.ShapeDtypeStruct((tok, width), F32),
            jax.ShapeDtypeStruct((1, 1), F32),
            *(jax.ShapeDtypeStruct(p.shape, F32) for p in params),
        ),
        in_specs=[smem] + [vmem] * 18,
        out_specs=(hbm, hbm, vmem) + (hbm,) * 15,
        scratch_shapes=[pltpu.VMEM(p.shape, F32) for p in params]
        + [pltpu.SemaphoreType.DMA((17,))],
        compiler_params=pltpu.CompilerParams(vmem_limit_bytes=16 * 2**20),
    )(step, output, input_grad, sums, *held)
    news = list(results[3:])
    for index in range(3):
        news[index] = flip(news[index])
    return (results[0], results[1], results[2].reshape(1), *news)


def solution(mesh):
    split = P(("dp", "mp"), None)
    in_specs = (
        split,
        P("dp", None),
        split,
        P(None, None, "mp"),
        P(None, "mp"),
        P("mp", None),
        P(),
        P(None, "mp"),
        P("mp"),
        P("mp", None),
    ) + (P(),) * 16
    out_specs = (split, split) + (P(),) * 16
    return jax.shard_map(
        functools.partial(per_device, mesh.shape["dp"]),
        mesh=mesh,
        in_specs=in_specs,
        out_specs=out_specs,
        check_vma=False,
    )
```

```python
import functools
import types

import jax
import jax.numpy as jnp
from jax import lax
from jax.experimental import pallas as pl
from jax.experimental.pallas import tpu as pltpu
from jax.sharding import PartitionSpec as P

HEAD_DIM = 64
SLOTS = 8
EPSILON = 1e-12
CLIP_LIMIT = 1.0
LOG2E = 1.4426950408889634
HALF_ROOT = 0.7071067811865476
DENSITY = 0.3989422804014327
NEGATIVE = -1e30
RATES = ((0.03, 0.01), (0.1, 0.0), (0.1, 0.01), (0.1, 0.0), (0.2, 0.0))
PART = 80
MESH = pl.DeviceIdType.MESH
BF = jnp.bfloat16
F32 = jnp.float32


def nn(a, b):
    return lax.dot_general(a, b, (((1,), (0,)), ((), ())), preferred_element_type=F32)


def nt(a, b):
    return lax.dot_general(a, b, (((1,), (1,)), ((), ())), preferred_element_type=F32)


def tn(a, b):
    return lax.dot_general(a, b, (((0,), (0,)), ((), ())), preferred_element_type=F32)


def at(start, size, step=None):
    if isinstance(start, int):
        return pl.ds(start, size)
    return pl.ds(pl.multiple_of(start, step or size), size)


def gelu_parts(value):
    mass = 0.5 + 0.5 * lax.erf(value * HALF_ROOT)
    slope = mass + value * (jnp.exp2(value * value * (-0.5 * LOG2E)) * DENSITY)
    return value * mass, slope


def fold_rows(value):
    rows, width = value.shape
    return jnp.sum(value.reshape(rows // 8, 8, width), axis=0)


SCRATCH = (
    ("xs", lambda z: ((z.tok, z.width), BF)),
    ("cots", lambda z: ((z.tok, z.width), BF)),
    ("w3", lambda z: ((z.width, 6 * z.half), BF)),
    ("wo", lambda z: ((2 * z.half, z.width), BF)),
    ("we", lambda z: ((z.width, z.ff), BF)),
    ("ws", lambda z: ((z.ff, z.width), BF)),
    ("down_l", lambda z: ((2, 64, z.width), BF)),
    ("up_l", lambda z: ((2, 64, z.width), BF)),
    ("bias_own", lambda z: ((8, z.ff_half), F32)),
    ("bias_far", lambda z: ((8, z.ff_half), F32)),
    ("keys", lambda z: ((z.tok, z.width), BF)),
    ("values", lambda z: ((z.tok, z.width), BF)),
    ("q_t", lambda z: ((z.width, z.tok), BF)),
    ("k_t", lambda z: ((z.width, z.tok), BF)),
    ("v_t", lambda z: ((z.width, z.tok), BF)),
    ("hot", lambda z: ((z.tok, 128), BF)),
    ("qa", lambda z: ((4 * 256, z.tok), BF)),
    ("ex", lambda z: ((z.heads, z.tok, z.tok), BF)),
    ("fac", lambda z: ((z.heads, 8, z.tok), F32)),
    ("o_t", lambda z: ((z.width, z.tok), BF)),
    ("att", lambda z: ((z.tok, z.width), BF)),
    ("br_l", lambda z: ((2, z.tok, z.width), BF)),
    ("act", lambda z: ((2, z.tok, 128), BF)),
    ("gd", lambda z: ((2, z.tok, 64), F32)),
    ("inl", lambda z: ((z.tok, 64), BF)),
    ("normed", lambda z: ((z.tok, z.width), F32)),
    ("scale_s", lambda z: ((z.tok, 1), F32)),
    ("first_f", lambda z: ((z.tok, z.width), F32)),
    ("first_l", lambda z: ((z.tok, z.width), BF)),
    ("hid", lambda z: ((z.tok, z.ff), BF)),
    ("slope", lambda z: ((z.tok, z.ff), BF)),
    ("tmp", lambda z: ((z.tok, z.width), F32)),
    ("grads", lambda z: ((2, 2, PART, z.width), F32)),
    ("acc", lambda z: ((48, z.width), F32)),
    ("c_recv", lambda z: ((2, PART, z.width), F32)),
    ("rs_buf", lambda z: ((2, z.n_dp, z.piece, 128), BF)),
    ("rs_recv", lambda z: ((2, z.n_dp - 1, z.piece, 128), BF)),
    ("ag_buf", lambda z: ((2, z.n_dp, z.piece, 128), BF)),
    ("ag_far", lambda z: ((2, z.n_dp, z.piece, 128), BF)),
)
SEMAPHORES = (
    ("load_sem", 25),
    ("meet", 0),
    ("far_send", 7),
    ("far_recv", 7),
    ("core_send", 4),
    ("core_recv", 4),
    ("ring_send", 4),
    ("ring_recv", 4),
)
INPUTS = (
    ("lengths", "s"),
    ("qv_bias", "v"),
    ("branch_bias", "v"),
    ("expand_bias", "v"),
    ("tokens", "h"),
    ("cot", "h"),
    ("triple", "h"),
    ("out_w", "h"),
    ("expand", "h"),
    ("shrink", "h"),
    *((f"param{index}", "h") for index in range(15)),
)
CHUNK = 256
SUB = 32


def weave(*works):
    queues = [[list(work), 0] for work in works]
    most = max(len(queue[0]) for queue in queues)
    for tick in range(most):
        for queue in queues:
            units, done = queue
            goal = -(-len(units) * (tick + 1) // most)
            for unit in units[done:goal]:
                unit()
            queue[1] = max(done, goal)


def normalize(v):
    center = v - jnp.mean(v, axis=-1, keepdims=True)
    scale = lax.rsqrt(jnp.mean(center * center, axis=-1, keepdims=True) + EPSILON)
    return center * scale, scale


def set_masks(z, r, ends):
    def marks(shape, axis):
        place = lax.broadcasted_iota(jnp.int32, shape, axis)
        found = jnp.zeros(shape, jnp.int32)
        for end in ends:
            found = found + (place >= end).astype(jnp.int32)
        return found

    tok = z.tok
    r.hot[...] = jnp.where(
        marks((tok, 128), 0) == lax.broadcasted_iota(jnp.int32, (tok, 128), 1), 1.0, 0.0
    ).astype(BF)
    shut = jnp.where(
        marks((128, tok), 1) == lax.broadcasted_iota(jnp.int32, (128, tok), 0), 0.0, NEGATIVE
    ).astype(BF)
    for slot in range(4):
        r.qa[at(slot * 256, 128), :] = jnp.zeros((128, tok), BF)
        r.qa[at(slot * 256 + 128, 128), :] = shut


def project(z, r, side):
    bias = (r.bias_own, r.bias_far)[side]
    base = side * 3 * z.half
    for n in range(0, 3 * z.half, 256):

        def unit(n=n):
            size = min(256, 3 * z.half - n)
            mixed = nn(r.xs[...], r.w3[:, at(base + n, size)])
            for start in range(n, n + size, 128):
                c, col = start // z.half, start % z.half
                part = mixed[:, start - n : start - n + 128]
                if c != 1:
                    part = part + bias[c // 2 : c // 2 + 1, at(col, 128)]
                low = part.astype(BF)
                place = at(side * z.half + col, 128)
                if c == 0:
                    r.q_t[place, :] = (low.astype(F32) * (HEAD_DIM ** -0.5)).astype(BF).T
                if c == 1:
                    r.keys[:, place] = low
                    r.k_t[place, :] = low.T
                if c == 2:
                    r.values[:, place] = low
                    r.v_t[place, :] = low.T

        yield unit


def attend(z, r, side):
    span = z.tok // 2
    first = side * z.half // HEAD_DIM
    count = z.half // HEAD_DIM
    ones = jnp.ones((16, z.tok), BF)
    kept = {}

    def score(head, kh, c):
        slot = head % 4
        if kh == 0 and c == 0:
            r.qa[at(slot * 256 + head % 2 * 64, 64), :] = r.q_t[at(head * 64, 64), :]
        part = at(kh * span, span)
        keys = jnp.concatenate([r.keys[part, at(head // 2 * 128, 128)], r.hot[part, :]], axis=1)
        return nn(keys, r.qa[at(slot * 256, 256), at(c * span, span)])

    def exponents(head, kh, c, s):
        top = jnp.max(s, axis=0, keepdims=True) * LOG2E
        r.ex[head, at(kh * span, span), at(c * span, span)] = jnp.exp2(s * LOG2E - top).astype(BF)
        kept[head, kh, c] = top

    def gather(head):
        rows = at(head * 64, 64)
        values = jnp.concatenate([r.v_t[rows, :], ones], axis=0)
        parts = [
            nn(values[:, kh * span : (kh + 1) * span], r.ex[head, at(kh * span, span), :])
            for kh in range(2)
        ]
        peaks = [
            jnp.concatenate([kept.pop((head, kh, c)) for c in range(2)], axis=1) for kh in range(2)
        ]
        peak = jnp.maximum(peaks[0], peaks[1])
        weights = [jnp.exp2(p - peak) for p in peaks]
        inverse = 1.0 / (parts[0][64:65] * weights[0] + parts[1][64:65] * weights[1])
        weights = [w * inverse for w in weights]
        r.fac[head, 0:1, :] = weights[0]
        r.fac[head, 1:2, :] = weights[1]
        r.o_t[rows, :] = (parts[0][:64] * weights[0] + parts[1][:64] * weights[1]).astype(BF)
        if head % 2:
            cols = at(head // 2 * 128, 128)
            r.att[:, cols] = r.o_t[cols, :].T

    units = [(head, kh, c) for head in range(first, first + count) for kh in range(2) for c in range(2)]
    ahead = []
    yield lambda: ahead.append(score(*units[0]))
    for index, unit in enumerate(units):

        def step(index=index, unit=unit):
            s = ahead.pop()
            if index + 1 < len(units):
                ahead.append(score(*units[index + 1]))
            exponents(*unit, s)
            if unit[1:] == (1, 1) and unit[0] > first:
                gather(unit[0] - 1)

        yield step
    yield lambda: gather(first + count - 1)


def big_dot(z, base, left, right, form, finish):
    rows = at(base, CHUNK)
    for n in range(0, z.width, 256):

        def unit(n=n):
            cols = at(n, 256)
            weights = right[:, cols] if form is nn else right[cols, :]
            finish(rows, cols, form(left[rows, :], weights))

        yield unit


def branch_out(z, r, index, base, left, right, before):
    def finish(rows, cols, product):
        value = product + r.branch_bias[index : index + 1, cols].astype(F32)
        r.br_l[index, rows, cols] = value.astype(BF)
        r.tmp[rows, cols] = value + before[rows, cols].astype(F32)

    return big_dot(z, base, left, right, nn, finish)


def shrink_own(z, r, base):
    rows = at(base, CHUNK)
    for n in range(0, z.width, 256):

        def unit(n=n):
            own = at(0, z.ff_half)
            r.tmp[rows, at(n, 256)] = nn(r.hid[rows, own], r.ws[own, at(n, 256)])

        yield unit


def shrink_far(z, r, base):
    def finish(rows, cols, product):
        value = product + r.tmp[rows, cols] + r.branch_bias[1:2, cols].astype(F32)
        r.br_l[1, rows, cols] = value.astype(BF)
        r.tmp[rows, cols] = value + r.first_f[rows, cols]

    far = at(z.ff_half, z.ff_half)
    return big_dot(z, base, r.hid.at[:, far], r.ws.at[far, :], nn, finish)


def adapt(z, r, index, base):
    def inner():
        rows = at(base, CHUNK)
        value, grade = gelu_parts(
            nt(r.br_l[index, rows, :], r.down_l[index]) + r.down_bias[index : index + 1, :]
        )
        low = value.astype(BF)
        r.act[index, rows, 0:64] = low
        r.gd[index, rows, :] = grade
        for n in range(0, z.width, 256):
            cols = at(n, 256)
            r.tmp[rows, cols] += nn(low, r.up_l[index, :, cols]) + r.up_bias[index : index + 1, cols]

    yield inner


def first_norm(z, r, base):
    yield from adapt(z, r, 0, base)
    for row in range(base, base + CHUNK, SUB):

        def unit(row=row):
            rows = at(row, SUB)
            normed, scale = normalize(r.tmp[rows, :])
            r.normed[rows, :] = normed
            r.scale_s[rows, :] = scale
            first = normed * r.norms[0:1, :] + r.norms[1:2, :]
            r.first_f[rows, :] = first
            r.first_l[rows, :] = first.astype(BF)

        yield unit


def expand(z, r, side, base):
    bias = (r.bias_own, r.bias_far)[side]
    rows = at(base, CHUNK)
    for j in range(0, z.ff_half, 256):

        def unit(j=j):
            cols = at(side * z.ff_half + j, 256)
            before = nn(r.first_l[rows, :], r.we[:, cols]) + bias[2:3, at(j, 256)]
            value, grade = gelu_parts(before)
            r.hid[rows, cols] = value.astype(BF)
            r.slope[rows, cols] = grade.astype(BF)

        yield unit


def unshrink(z, r, base):
    rows = at(base, CHUNK)
    for j in range(0, z.ff, 256):

        def unit(j=j):
            cols = at(j, 256)
            grad = nt(r.sgl[rows, :], r.ws[cols, :])
            r.hid[rows, cols] = (grad * r.slope[rows, cols].astype(F32)).astype(BF)

        yield unit


def norm_back(sums, grad, unit, scale, gain):
    for place, part in enumerate((fold_rows(grad * unit), fold_rows(grad))):
        sums[place] = part if sums[place] is None else sums[place] + part
    inner = grad * gain
    back = scale * (
        inner
        - jnp.mean(inner, axis=-1, keepdims=True)
        - unit * jnp.mean(inner * unit, axis=-1, keepdims=True)
    )
    return back, back.astype(BF)


def adapter_out(z, r, index, base, sums):
    def inner():
        rows = at(base, CHUNK)
        low = (nt(r.gl[rows, :], r.up_l[index]) * r.gd[index, rows, :]).astype(BF)
        r.inl[rows, :] = low
        for n in range(0, z.width, 256):
            cols = at(n, 256)
            r.sgl[rows, cols] = (r.ssg[rows, cols] + nn(low, r.down_l[index, :, cols])).astype(BF)
        for place in range(2):
            lines = at((2 * index + place) * 8, 8)
            r.acc[lines, :] = sums[place] if base == 0 else r.acc[lines, :] + sums[place]

    yield inner


def second_norm(z, r, base):
    yield from adapt(z, r, 1, base)
    sums = [None, None]
    for row in range(base, base + CHUNK, SUB):

        def unit(row=row):
            rows = at(row, SUB)
            normed, scale = normalize(r.tmp[rows, :])
            r.output[rows, :] = normed * r.norms[2:3, :] + r.norms[3:4, :]
            back, low = norm_back(
                sums, r.cots[rows, :].astype(F32), normed, scale, r.norms[2:3, :]
            )
            r.ssg[rows, :] = back
            r.gl[rows, :] = low

        yield unit
    yield from adapter_out(z, r, 1, base, sums)


def first_out(z, r, base):
    def finish(rows, cols, product):
        r.tmp[rows, cols] = product + r.ssg[rows, cols]

    return big_dot(z, base, r.hid, r.we, nt, finish)


def first_back(z, r, base):
    sums = [None, None]
    for row in range(base, base + CHUNK, SUB):

        def unit(row=row):
            rows = at(row, SUB)
            back, low = norm_back(
                sums, r.tmp[rows, :], r.normed[rows, :], r.scale_s[rows, :], r.norms[0:1, :]
            )
            r.ssg[rows, :] = back
            r.gl[rows, :] = low

        yield unit
    yield from adapter_out(z, r, 0, base, sums)


def collect(z, r, index):
    def down():
        r.grads[index, 0, 0:64, :] = tn(r.inl[...], r.br_l[index])

    def up():
        r.grads[index, 1, 0:72, :] = tn(r.act[index], r.gl[...])[0:72]

    def lines():
        for place in range(2):
            line = jnp.sum(r.acc[at((2 * index + place) * 8, 8), :], axis=0, keepdims=True)
            r.grads[index, 0, 64 + place : 65 + place, :] = line
        r.grads[index, 1, 65:66, 0:64] = jnp.sum(r.inl[...].astype(F32), axis=0, keepdims=True)

    yield down
    yield up
    yield lines


def branch_back(z, r, base):
    for row in range(0, z.width, 256):

        def unit(row=row):
            rows = at(row, 256)
            r.dat[rows, at(base, CHUNK)] = nt(r.wo[rows, :], r.sgl[at(base, CHUNK), :]).astype(BF)

        yield unit


def attend_back(z, r, pair):
    span = z.tok // 2
    cols = at(pair * 128, 128)
    values = r.values[:, cols]
    got = [[], [], []]
    for j in range(2):
        head = pair * 2 + j
        rows = at(pair * 128 + j * 64, 64)
        grad = r.dat[rows, :].astype(F32)
        dot = jnp.sum(grad * r.o_t[rows, :].astype(F32), axis=0, keepdims=True)
        score_grads = []
        value_grads = []
        for kh in range(2):
            weight = r.fac[head, kh : kh + 1, :]
            scaled = (grad * weight).astype(BF)
            pieces = [scaled, jnp.zeros((64, z.tok), BF)]
            spread = jnp.concatenate(pieces if j == 0 else pieces[::-1], axis=0)
            back = nn(values[kh * span : (kh + 1) * span], spread)
            exps = r.ex[head, at(kh * span, span), :]
            score_grads.append((exps.astype(F32) * (back - dot * weight)).astype(BF))
            value_grads.append(nt(scaled, exps))
        scores = jnp.concatenate(score_grads, axis=0)
        got[0].append((nn(r.k_t[rows, :], scores) * (HEAD_DIM ** -0.5)).astype(BF))
        got[1].append(nt(r.q_t[rows, :], scores).astype(BF))
        got[2].append(jnp.concatenate(value_grads, axis=1).astype(BF))
    pairs_half = z.half // 128
    side = lax.div(pair, pairs_half)
    offset = side * 3 * z.half + lax.rem(pair, pairs_half) * 128
    for c in range(3):
        r.dqkv[:, at(offset + c * z.half, 128)] = jnp.concatenate(got[c], axis=0).T


def input_back(z, r, base):
    rows = at(base, CHUNK)
    r.input_grad[rows, :] = r.ssg[rows, :] + nt(r.dqkv[rows, 0 : 6 * z.half], r.w3[...])


def share(r):
    r.dqkv, r.dat, r.sgl, r.gl, r.ssg = r.slope, r.v_t, r.first_l, r.att, r.first_f


def layer_kernel(z, *refs):
    names = [name for name, _ in INPUTS] + ["output", "input_grad", "sums"]
    names += [f"held{index}" for index in range(15)]
    names += [name for name, _ in SCRATCH] + [name for name, _ in SEMAPHORES]
    r = types.SimpleNamespace(**dict(zip(names, refs, strict=True)))
    share(r)
    r.down_bias, r.up_bias, r.norms = r.held3, r.held9, r.held12
    tok, width, half, ff_half, n_dp, piece = z.tok, z.width, z.half, z.ff_half, z.n_dp, z.piece
    wide = 3 * half
    dp = lax.axis_index("dp")
    mp = lax.axis_index("mp")
    mate = (dp, 1 - mp)

    def load(src, dst, index):
        copy = pltpu.make_async_copy(src, dst, r.load_sem.at[index])
        copy.start()
        return copy

    load_x = load(r.tokens, r.xs, 0)
    load_w3 = [load(r.triple.at[c], r.w3.at[:, at(c * half, half)], 1 + c) for c in range(3)]

    barrier = pltpu.get_barrier_semaphore()
    ready, go = r.meet.at[0], r.meet.at[1]

    @pl.when(mp == 0)
    def call():
        pl.semaphore_signal(barrier, inc=1, device_id=mate, device_id_type=MESH)

    r.bias_own[...] = jnp.zeros_like(r.bias_own)
    r.bias_own[0:2, 0:half] = r.qv_bias[...].astype(F32)
    r.bias_own[2:3, :] = r.expand_bias[...].astype(F32).reshape(1, ff_half)

    ends = []
    total = jnp.int32(0)
    for slot in range(SLOTS - 1):
        total = total + jnp.where(mp == 0, r.lengths[0, slot], r.lengths[1, slot])
        ends.append(total)

    @pl.when(mp == 1)
    def answer():
        pl.semaphore_wait(barrier, 1)
        pl.semaphore_signal(ready, inc=1, device_id=mate, device_id_type=MESH)

    @pl.when(mp == 0)
    def hear():
        pl.semaphore_wait(ready, 1)

        def greet(step, carry):
            peer = lax.rem(dp + step, n_dp)
            pl.semaphore_signal(barrier, inc=1, device_id=(peer, mp), device_id_type=MESH)
            return carry

        lax.fori_loop(1, n_dp, greet, 0)

    def gather_all():
        @pl.when(mp == 0)
        def first_core():
            pl.semaphore_wait(barrier, n_dp - 1)
            pl.semaphore_signal(go, inc=1, device_id=mate, device_id_type=MESH)

        @pl.when(mp == 1)
        def second_core():
            pl.semaphore_wait(go, 1)

    def push(src, dst, index):
        copy = pltpu.make_async_remote_copy(
            src_ref=src,
            dst_ref=dst,
            send_sem=r.far_send.at[index],
            recv_sem=r.far_recv.at[index],
            device_id=mate,
            device_id_type=MESH,
        )
        copy.start()
        return copy

    far_bias = push(r.bias_own, r.bias_far, 0)
    far_w3 = [
        push(r.triple.at[c], r.w3.at[:, at(wide + c * half, half)], 1 + c) for c in range(3)
    ]
    set_masks(z, r, ends)
    r.grads[...] = jnp.zeros_like(r.grads)
    marker = lax.broadcasted_iota(jnp.int32, (tok, 128), 1) == 64
    for index in range(2):
        r.act[index] = jnp.where(marker, 1.0, 0.0).astype(BF)
    load_x.wait()
    for copy in load_w3:
        copy.wait()
    load_down = load(r.param0, r.held0, 4)
    load_up = load(r.param6, r.held6, 5)
    load_small = [
        load(getattr(r, f"param{index}"), getattr(r, f"held{index}"), 10 + index)
        for index in (3, 9, 12)
    ]
    load_wo = load(r.out_w, r.wo.at[at(0, half), :], 6)
    load_we = load(r.expand, r.we.at[:, at(0, ff_half)], 7)
    load_ws = load(r.shrink, r.ws.at[at(0, ff_half), :], 8)
    load_cot = load(r.cot, r.cots, 9)
    weave(project(z, r, 0))
    far_wo = push(r.out_w, r.wo.at[at(half, half), :], 4)
    far_we = push(r.expand, r.we.at[:, at(ff_half, ff_half)], 5)
    weave(attend(z, r, 0))
    far_ws = push(r.shrink, r.ws.at[at(ff_half, ff_half), :], 6)
    far_bias.wait()
    for copy in far_w3:
        copy.wait()
    weave(project(z, r, 1))
    weave(attend(z, r, 1))

    load_down.wait()
    load_up.wait()
    r.down_l[...] = r.held0[...].astype(BF)
    r.up_l[...] = r.held6[...].astype(BF)
    held = [
        load(getattr(r, f"param{index}"), getattr(r, f"held{index}"), 10 + index)
        for index in range(15)
        if index not in (0, 3, 6, 9, 12)
    ]
    for copy in load_small:
        copy.wait()
    load_wo.wait()
    far_wo.wait()
    load_we.wait()

    def core_copy(b):
        return pltpu.make_async_remote_copy(
            src_ref=r.grads.at[b, 1 - mp],
            dst_ref=r.c_recv.at[b],
            send_sem=r.core_send.at[2 * b],
            recv_sem=r.core_recv.at[2 * b],
            device_id=mate,
            device_id_type=MESH,
        )

    def ring_start(b, stage):
        def body(step, carry):
            peer = lax.rem(dp + step, n_dp)
            if stage == 0:
                src, dst = r.rs_buf.at[b, peer], r.rs_recv.at[b, step - 1]
            else:
                src, dst = r.ag_buf.at[b, dp], r.ag_buf.at[b, dp]
            pltpu.make_async_remote_copy(
                src_ref=src,
                dst_ref=dst,
                send_sem=r.ring_send.at[2 * b + stage],
                recv_sem=r.ring_recv.at[2 * b + stage],
                device_id=(peer, mp),
                device_id_type=MESH,
            ).start()
            return carry

        lax.fori_loop(1, n_dp, body, 0)

    def ring_wait(b, stage):
        block = r.rs_recv.at[b]
        pltpu.make_async_copy(block, block, r.ring_send.at[2 * b + stage]).wait()
        pltpu.make_async_copy(block, block, r.ring_recv.at[2 * b + stage]).wait()

    def last_copy(b):
        return pltpu.make_async_remote_copy(
            src_ref=r.ag_buf.at[b],
            dst_ref=r.ag_far.at[b],
            send_sem=r.core_send.at[2 * b + 1],
            recv_sem=r.core_recv.at[2 * b + 1],
            device_id=mate,
            device_id_type=MESH,
        )

    def reduce_one(b):
        core_copy(b).start()

    def reduce_two(b):
        core_copy(b).wait()
        mine = (r.grads[b, mp] + r.c_recv[b]).astype(BF)
        blocks = jnp.concatenate(
            [mine[:, c * 128 : (c + 1) * 128] for c in range(width // 128)], axis=0
        )
        spare = n_dp * piece - blocks.shape[0]
        if spare:
            blocks = jnp.concatenate([blocks, jnp.zeros((spare, 128), BF)], axis=0)
        r.rs_buf[b] = blocks.reshape(n_dp, piece, 128)
        ring_start(b, 0)

    def reduce_three(b):
        ring_wait(b, 0)
        total = jnp.sum(r.rs_recv[b].astype(F32), axis=0) + r.rs_buf[b, dp].astype(F32)
        r.ag_buf[b, dp] = total.astype(BF)
        ring_start(b, 1)

    def reduce_four(b):
        ring_wait(b, 1)
        last_copy(b).start()

    def reduce_five(b):
        last_copy(b).wait()

    late = CHUNK
    att = r.att
    weave(branch_out(z, r, 0, 0, att, r.wo, r.xs))
    weave(branch_out(z, r, 0, late, att, r.wo, r.xs), first_norm(z, r, 0))
    weave(expand(z, r, 0, 0), first_norm(z, r, late))
    weave(expand(z, r, 0, late))
    load_ws.wait()
    weave(shrink_own(z, r, 0))
    weave(shrink_own(z, r, late))
    gather_all()
    load_cot.wait()
    far_we.wait()
    weave(expand(z, r, 1, 0))
    far_ws.wait()
    weave(shrink_far(z, r, 0))
    weave([*expand(z, r, 1, late), *shrink_far(z, r, late)], second_norm(z, r, 0))
    weave(unshrink(z, r, 0), second_norm(z, r, late))
    weave(unshrink(z, r, late), collect(z, r, 1))
    reduce_one(1)
    weave(first_out(z, r, 0))
    weave(first_out(z, r, late), first_back(z, r, 0))
    reduce_two(1)
    weave(branch_back(z, r, 0), first_back(z, r, late))
    weave(collect(z, r, 0))
    reduce_one(0)
    weave(branch_back(z, r, late))

    def back(pair, carry):
        attend_back(z, r, pair)
        return carry

    pairs = width // 128
    middle = pairs // 2
    lax.fori_loop(0, 1, back, 0)
    reduce_two(0)
    lax.fori_loop(1, middle, back, 0)
    reduce_three(1)
    lax.fori_loop(middle, pairs, back, 0)
    reduce_three(0)
    for base in range(0, tok, CHUNK):
        input_back(z, r, base)
    reduce_four(1)
    for copy in held:
        copy.wait()
    reduce_five(1)
    reduce_four(0)
    for b in range(2):
        r.sums[b, mp] = r.ag_buf[b]
    r.sums[1, 1 - mp] = r.ag_far[1]
    reduce_five(0)
    r.sums[0, 1 - mp] = r.ag_far[0]


def update_kernel(blocks, step, output_src, input_grad_src, sums, *refs):
    params, rest = refs[:15], refs[15:]
    output, input_grad, norm_out = rest[:3]
    targets, news, sem = rest[3:18], rest[18:33], rest[33]
    stores = []

    def store(src, dst):
        copy = pltpu.make_async_copy(src, dst, sem.at[len(stores)])
        copy.start()
        stores.append(copy)

    store(output_src, output)
    store(input_grad_src, input_grad)
    squares = jnp.zeros((8, 128), F32)
    for b in range(2):
        for side in range(2):
            part = sums[b, side].astype(F32)
            squares = squares + fold_rows(part * part)
    squares = jnp.sum(jnp.sum(squares, axis=0, keepdims=True), axis=1, keepdims=True)
    grad_norm = jnp.sqrt(squares)
    norm_out[...] = grad_norm
    clip = jnp.minimum(1.0, CLIP_LIMIT / (grad_norm + 1e-06))
    count = jnp.full((1, 1), step[0], jnp.int32).astype(F32)
    fix_one = 1.0 - jnp.exp2(count * jnp.log2(jnp.full((1, 1), 0.9, F32)))
    fix_two = 1.0 - jnp.exp2(count * jnp.log2(jnp.full((1, 1), 0.999, F32)))
    over_one = 1.0 / fix_one
    over_two = 1.0 / fix_two

    def update(index, where, grad):
        weight, first, second = (params[3 * index + n][where] for n in range(3))
        rate, decay = RATES[index]
        clipped = grad * clip
        first_new = 0.9 * first + 0.1 * clipped
        second_new = 0.999 * second + 0.001 * clipped * clipped
        square = second_new * over_two
        root = square * lax.rsqrt(square) + 1e-08
        guess = pltpu.reciprocal(root, approx=True)
        move = first_new * over_one * (guess * (2.0 - root * guess))
        if decay:
            move = move + decay * weight
        news[3 * index][where] = weight - rate * move
        news[3 * index + 1][where] = first_new
        news[3 * index + 2][where] = second_new

    lines = {}
    for side in range(2):
        for b in range(2):
            tops = []
            for c in range(blocks):
                block = sums[b, side, pl.ds(c * PART, PART), :].astype(F32)
                update(2 * side, (b, slice(None), slice(c * 128, (c + 1) * 128)), block[0:64])
                tops.append(block[64:72])
            lines[b, side] = jnp.concatenate(tops, axis=1)
        for n in range(3):
            store(news[6 * side + n], targets[6 * side + n])
    for b in range(2):
        update(4, (slice(2 * b, 2 * b + 2), slice(None)), lines[b, 0][0:2])
        update(3, (slice(b, b + 1), slice(None)), lines[b, 1][0:1])
        update(1, (slice(b, b + 1), slice(None)), lines[b, 1][1:2, 0:64])
    for index in (3, 4, 5, 9, 10, 11, 12, 13, 14):
        store(news[index], targets[index])
    for copy in stores:
        copy.wait()


def per_device(
    n_dp,
    tokens,
    lengths,
    cotangent,
    triple_weight,
    query_value_bias,
    output_weight,
    branch_bias,
    expand_weight,
    expand_bias,
    shrink_weight,
    adapter_down,
    down_bias,
    adapter_up,
    up_bias,
    norm_params,
    adapter_down_first,
    adapter_down_second,
    down_bias_first,
    down_bias_second,
    adapter_up_first,
    adapter_up_second,
    up_bias_first,
    up_bias_second,
    norm_params_first,
    norm_params_second,
    step,
):
    tok, width = tokens.shape
    half = triple_weight.shape[2]
    ff_half = expand_weight.shape[1]
    ff = 2 * ff_half
    heads = 2 * half // HEAD_DIM
    blocks = width // 128
    piece = -(-(PART * blocks) // (16 * n_dp)) * 16
    z = types.SimpleNamespace(
        tok=tok,
        width=width,
        half=half,
        ff_half=ff_half,
        ff=ff,
        heads=heads,
        n_dp=n_dp,
        piece=piece,
    )
    flip = lambda v: jnp.swapaxes(v, 1, 2)
    spaces = {
        "s": pl.BlockSpec(memory_space=pltpu.SMEM),
        "v": pl.BlockSpec(memory_space=pltpu.VMEM),
        "h": pl.BlockSpec(memory_space=pltpu.HBM),
    }
    vmem, smem, hbm = spaces["v"], spaces["s"], spaces["h"]
    params = (
        flip(adapter_down),
        flip(adapter_down_first),
        flip(adapter_down_second),
        down_bias,
        down_bias_first,
        down_bias_second,
        adapter_up,
        adapter_up_first,
        adapter_up_second,
        up_bias,
        up_bias_first,
        up_bias_second,
        norm_params,
        norm_params_first,
        norm_params_second,
    )
    operands = (
        lengths,
        query_value_bias,
        branch_bias,
        expand_bias,
        tokens,
        cotangent,
        jnp.transpose(triple_weight, (1, 0, 2)),
        output_weight,
        expand_weight,
        shrink_weight,
        *params,
    )
    output, input_grad, sums, *held = pl.pallas_call(
        functools.partial(layer_kernel, z),
        out_shape=(
            pltpu.VMEM((tok, width), F32),
            pltpu.VMEM((tok, width), F32),
            pltpu.VMEM((2, 2, n_dp, piece, 128), BF),
            *(pltpu.VMEM(p.shape, F32) for p in params),
        ),
        in_specs=[spaces[space] for _, space in INPUTS],
        out_specs=(vmem,) * 18,
        scratch_shapes=[pltpu.VMEM(*make(z)) for _, make in SCRATCH]
        + [
            pltpu.SemaphoreType.DMA((count,)) if count else pltpu.SemaphoreType.REGULAR((2,))
            for _, count in SEMAPHORES
        ],
        compiler_params=pltpu.CompilerParams(
            collective_id=0, has_side_effects=True, vmem_limit_bytes=56 * 2**20
        ),
    )(*operands)
    sums = sums.reshape(2, 2, n_dp * piece, 128)
    results = pl.pallas_call(
        functools.partial(update_kernel, blocks),
        out_shape=(
            jax.ShapeDtypeStruct((tok, width), F32),
            jax.ShapeDtypeStruct((tok, width), F32),
            jax.ShapeDtypeStruct((1, 1), F32),
            *(jax.ShapeDtypeStruct(p.shape, F32) for p in params),
        ),
        in_specs=[smem] + [vmem] * 18,
        out_specs=(hbm, hbm, vmem) + (hbm,) * 15,
        scratch_shapes=[pltpu.VMEM(p.shape, F32) for p in params]
        + [pltpu.SemaphoreType.DMA((17,))],
        compiler_params=pltpu.CompilerParams(vmem_limit_bytes=16 * 2**20),
    )(step, output, input_grad, sums, *held)
    news = list(results[3:])
    for index in range(3):
        news[index] = flip(news[index])
    return (results[0], results[1], results[2].reshape(1), *news)


def solution(mesh):
    split = P(("dp", "mp"), None)
    in_specs = (
        split,
        P("dp", None),
        split,
        P(None, None, "mp"),
        P(None, "mp"),
        P("mp", None),
        P(),
        P(None, "mp"),
        P("mp"),
        P("mp", None),
    ) + (P(),) * 16
    out_specs = (split, split) + (P(),) * 16
    return jax.shard_map(
        functools.partial(per_device, mesh.shape["dp"]),
        mesh=mesh,
        in_specs=in_specs,
        out_specs=out_specs,
        check_vma=False,
    )
```

```python
import functools
import types

import jax
import jax.numpy as jnp
from jax import lax
from jax.experimental import pallas as pl
from jax.experimental.pallas import tpu as pltpu
from jax.sharding import PartitionSpec as P

HEAD_DIM = 64
SLOTS = 8
EPSILON = 1e-12
CLIP_LIMIT = 1.0
LOG2E = 1.4426950408889634
HALF_ROOT = 0.7071067811865476
DENSITY = 0.3989422804014327
NEGATIVE = -1e30
RATES = ((0.03, 0.01), (0.1, 0.0), (0.1, 0.01), (0.1, 0.0), (0.2, 0.0))
PART = 80
MESH = pl.DeviceIdType.MESH
BF = jnp.bfloat16
F32 = jnp.float32


def nn(a, b):
    return lax.dot_general(a, b, (((1,), (0,)), ((), ())), preferred_element_type=F32)


def nt(a, b):
    return lax.dot_general(a, b, (((1,), (1,)), ((), ())), preferred_element_type=F32)


def tn(a, b):
    return lax.dot_general(a, b, (((0,), (0,)), ((), ())), preferred_element_type=F32)


def at(start, size, step=None):
    if isinstance(start, int):
        return pl.ds(start, size)
    return pl.ds(pl.multiple_of(start, step or size), size)


def gelu_parts(value):
    mass = 0.5 + 0.5 * lax.erf(value * HALF_ROOT)
    slope = mass + value * (jnp.exp2(value * value * (-0.5 * LOG2E)) * DENSITY)
    return value * mass, slope


def fold_rows(value):
    rows, width = value.shape
    return jnp.sum(value.reshape(rows // 8, 8, width), axis=0)


SCRATCH = (
    ("qv_bias", lambda z: ((2, z.half), BF)),
    ("branch_bias", lambda z: ((2, z.width), BF)),
    ("expand_bias", lambda z: ((z.ff_half,), BF)),
    ("xs", lambda z: ((z.tok, z.width), BF)),
    ("cots", lambda z: ((z.tok, z.width), BF)),
    ("w3", lambda z: ((z.width, 6 * z.half), BF)),
    ("wo", lambda z: ((2 * z.half, z.width), BF)),
    ("we", lambda z: ((z.width, z.ff), BF)),
    ("ws", lambda z: ((z.ff, z.width), BF)),
    ("down_l", lambda z: ((2, 64, z.width), BF)),
    ("up_l", lambda z: ((2, 64, z.width), BF)),
    ("bias_own", lambda z: ((8, z.ff_half), F32)),
    ("bias_far", lambda z: ((8, z.ff_half), F32)),
    ("keys", lambda z: ((z.tok, z.width), BF)),
    ("values", lambda z: ((z.tok, z.width), BF)),
    ("q_t", lambda z: ((z.width, z.tok), BF)),
    ("k_t", lambda z: ((z.width, z.tok), BF)),
    ("v_t", lambda z: ((z.width, z.tok), BF)),
    ("hot", lambda z: ((z.tok, 128), BF)),
    ("qa", lambda z: ((4 * 256, z.tok), BF)),
    ("ex", lambda z: ((z.heads, z.tok, z.tok), BF)),
    ("fac", lambda z: ((z.heads, 8, z.tok), F32)),
    ("o_t", lambda z: ((z.width, z.tok), BF)),
    ("att", lambda z: ((z.tok, z.width), BF)),
    ("br_l", lambda z: ((2, z.tok, z.width), BF)),
    ("act", lambda z: ((2, z.tok, 128), BF)),
    ("gd", lambda z: ((2, z.tok, 64), F32)),
    ("inl", lambda z: ((z.tok, 64), BF)),
    ("normed", lambda z: ((z.tok, z.width), F32)),
    ("scale_s", lambda z: ((z.tok, 1), F32)),
    ("first_f", lambda z: ((z.tok, z.width), F32)),
    ("first_l", lambda z: ((z.tok, z.width), BF)),
    ("hid", lambda z: ((z.tok, z.ff), BF)),
    ("slope", lambda z: ((z.tok, z.ff), BF)),
    ("tmp", lambda z: ((z.tok, z.width), F32)),
    ("grads", lambda z: ((2, 2, PART, z.width), F32)),
    ("acc", lambda z: ((48, z.width), F32)),
    ("c_recv", lambda z: ((2, PART, z.width), F32)),
    ("rs_buf", lambda z: ((2, z.n_dp, z.piece, 128), BF)),
    ("rs_recv", lambda z: ((2, z.n_dp - 1, z.piece, 128), BF)),
    ("ag_buf", lambda z: ((2, z.n_dp, z.piece, 128), BF)),
    ("ag_far", lambda z: ((2, z.n_dp, z.piece, 128), BF)),
)
SEMAPHORES = (
    ("load_sem", 29),
    ("meet", 0),
    ("far_send", 7),
    ("far_recv", 7),
    ("core_send", 4),
    ("core_recv", 4),
    ("ring_send", 4),
    ("ring_recv", 4),
)
INPUTS = (
    ("lengths_hbm", "h"),
    ("qv_hbm", "h"),
    ("branch_hbm", "h"),
    ("expand_b_hbm", "h"),
    ("tokens", "h"),
    ("cot", "h"),
    ("triple", "h"),
    ("out_w", "h"),
    ("expand", "h"),
    ("shrink", "h"),
    *((f"param{index}", "h") for index in range(15)),
)
CHUNK = 256
SUB = 32


def weave(*works):
    queues = [[list(work), 0] for work in works]
    most = max(len(queue[0]) for queue in queues)
    for tick in range(most):
        for queue in queues:
            units, done = queue
            goal = -(-len(units) * (tick + 1) // most)
            for unit in units[done:goal]:
                unit()
            queue[1] = max(done, goal)


def normalize(v):
    center = v - jnp.mean(v, axis=-1, keepdims=True)
    scale = lax.rsqrt(jnp.mean(center * center, axis=-1, keepdims=True) + EPSILON)
    return center * scale, scale


def set_masks(z, r, ends):
    def marks(shape, axis):
        place = lax.broadcasted_iota(jnp.int32, shape, axis)
        found = jnp.zeros(shape, jnp.int32)
        for end in ends:
            found = found + (place >= end).astype(jnp.int32)
        return found

    tok = z.tok
    r.hot[...] = jnp.where(
        marks((tok, 128), 0) == lax.broadcasted_iota(jnp.int32, (tok, 128), 1), 1.0, 0.0
    ).astype(BF)
    shut = jnp.where(
        marks((128, tok), 1) == lax.broadcasted_iota(jnp.int32, (128, tok), 0), 0.0, NEGATIVE
    ).astype(BF)
    for slot in range(4):
        r.qa[at(slot * 256, 128), :] = jnp.zeros((128, tok), BF)
        r.qa[at(slot * 256 + 128, 128), :] = shut


def project(z, r, side):
    bias = (r.bias_own, r.bias_far)[side]
    base = side * 3 * z.half
    for n in range(0, 3 * z.half, 256):

        def unit(n=n):
            size = min(256, 3 * z.half - n)
            mixed = nn(r.xs[...], r.w3[:, at(base + n, size)])
            for start in range(n, n + size, 128):
                c, col = start // z.half, start % z.half
                part = mixed[:, start - n : start - n + 128]
                if c != 1:
                    part = part + bias[c // 2 : c // 2 + 1, at(col, 128)]
                low = part.astype(BF)
                place = at(side * z.half + col, 128)
                if c == 0:
                    r.q_t[place, :] = (low.astype(F32) * (HEAD_DIM ** -0.5)).astype(BF).T
                if c == 1:
                    r.keys[:, place] = low
                    r.k_t[place, :] = low.T
                if c == 2:
                    r.values[:, place] = low
                    r.v_t[place, :] = low.T

        yield unit


def attend(z, r, side):
    span = z.tok // 2
    first = side * z.half // HEAD_DIM
    count = z.half // HEAD_DIM
    ones = jnp.ones((16, z.tok), BF)
    kept = {}

    def score(head, kh, c):
        slot = head % 4
        if kh == 0 and c == 0:
            r.qa[at(slot * 256 + head % 2 * 64, 64), :] = r.q_t[at(head * 64, 64), :]
        part = at(kh * span, span)
        keys = jnp.concatenate([r.keys[part, at(head // 2 * 128, 128)], r.hot[part, :]], axis=1)
        return nn(keys, r.qa[at(slot * 256, 256), at(c * span, span)])

    def exponents(head, kh, c, s):
        top = jnp.max(s, axis=0, keepdims=True) * LOG2E
        r.ex[head, at(kh * span, span), at(c * span, span)] = jnp.exp2(s * LOG2E - top).astype(BF)
        kept[head, kh, c] = top

    def gather(head):
        rows = at(head * 64, 64)
        values = jnp.concatenate([r.v_t[rows, :], ones], axis=0)
        parts = [
            nn(values[:, kh * span : (kh + 1) * span], r.ex[head, at(kh * span, span), :])
            for kh in range(2)
        ]
        peaks = [
            jnp.concatenate([kept.pop((head, kh, c)) for c in range(2)], axis=1) for kh in range(2)
        ]
        peak = jnp.maximum(peaks[0], peaks[1])
        weights = [jnp.exp2(p - peak) for p in peaks]
        inverse = 1.0 / (parts[0][64:65] * weights[0] + parts[1][64:65] * weights[1])
        weights = [w * inverse for w in weights]
        r.fac[head, 0:1, :] = weights[0]
        r.fac[head, 1:2, :] = weights[1]
        r.o_t[rows, :] = (parts[0][:64] * weights[0] + parts[1][:64] * weights[1]).astype(BF)
        if head % 2:
            cols = at(head // 2 * 128, 128)
            r.att[:, cols] = r.o_t[cols, :].T

    units = [(head, kh, c) for head in range(first, first + count) for kh in range(2) for c in range(2)]
    ahead = []
    yield lambda: ahead.append(score(*units[0]))
    for index, unit in enumerate(units):

        def step(index=index, unit=unit):
            s = ahead.pop()
            if index + 1 < len(units):
                ahead.append(score(*units[index + 1]))
            exponents(*unit, s)
            if unit[1:] == (1, 1) and unit[0] > first:
                gather(unit[0] - 1)

        yield step
    yield lambda: gather(first + count - 1)


def big_dot(z, base, left, right, form, finish):
    rows = at(base, CHUNK)
    for n in range(0, z.width, 256):

        def unit(n=n):
            cols = at(n, 256)
            weights = right[:, cols] if form is nn else right[cols, :]
            finish(rows, cols, form(left[rows, :], weights))

        yield unit


def branch_out(z, r, index, base, left, right, before):
    def finish(rows, cols, product):
        value = product + r.branch_bias[index : index + 1, cols].astype(F32)
        r.br_l[index, rows, cols] = value.astype(BF)
        r.tmp[rows, cols] = value + before[rows, cols].astype(F32)

    return big_dot(z, base, left, right, nn, finish)


def shrink_own(z, r, base):
    rows = at(base, CHUNK)
    for n in range(0, z.width, 256):

        def unit(n=n):
            own = at(0, z.ff_half)
            r.tmp[rows, at(n, 256)] = nn(r.hid[rows, own], r.ws[own, at(n, 256)])

        yield unit


def shrink_far(z, r, base):
    def finish(rows, cols, product):
        value = product + r.tmp[rows, cols] + r.branch_bias[1:2, cols].astype(F32)
        r.br_l[1, rows, cols] = value.astype(BF)
        r.tmp[rows, cols] = value + r.first_f[rows, cols]

    far = at(z.ff_half, z.ff_half)
    return big_dot(z, base, r.hid.at[:, far], r.ws.at[far, :], nn, finish)


def adapt(z, r, index, base):
    def inner():
        rows = at(base, CHUNK)
        value, grade = gelu_parts(
            nt(r.br_l[index, rows, :], r.down_l[index]) + r.down_bias[index : index + 1, :]
        )
        low = value.astype(BF)
        r.act[index, rows, 0:64] = low
        r.gd[index, rows, :] = grade
        for n in range(0, z.width, 256):
            cols = at(n, 256)
            r.tmp[rows, cols] += nn(low, r.up_l[index, :, cols]) + r.up_bias[index : index + 1, cols]

    yield inner


def first_norm(z, r, base):
    yield from adapt(z, r, 0, base)
    for row in range(base, base + CHUNK, SUB):

        def unit(row=row):
            rows = at(row, SUB)
            normed, scale = normalize(r.tmp[rows, :])
            r.normed[rows, :] = normed
            r.scale_s[rows, :] = scale
            first = normed * r.norms[0:1, :] + r.norms[1:2, :]
            r.first_f[rows, :] = first
            r.first_l[rows, :] = first.astype(BF)

        yield unit


def expand(z, r, side, base):
    bias = (r.bias_own, r.bias_far)[side]
    rows = at(base, CHUNK)
    for j in range(0, z.ff_half, 256):

        def unit(j=j):
            cols = at(side * z.ff_half + j, 256)
            before = nn(r.first_l[rows, :], r.we[:, cols]) + bias[2:3, at(j, 256)]
            value, grade = gelu_parts(before)
            r.hid[rows, cols] = value.astype(BF)
            r.slope[rows, cols] = grade.astype(BF)

        yield unit


def unshrink(z, r, base):
    rows = at(base, CHUNK)
    for j in range(0, z.ff, 256):

        def unit(j=j):
            cols = at(j, 256)
            grad = nt(r.sgl[rows, :], r.ws[cols, :])
            r.hid[rows, cols] = (grad * r.slope[rows, cols].astype(F32)).astype(BF)

        yield unit


def norm_back(sums, grad, unit, scale, gain):
    for place, part in enumerate((fold_rows(grad * unit), fold_rows(grad))):
        sums[place] = part if sums[place] is None else sums[place] + part
    inner = grad * gain
    back = scale * (
        inner
        - jnp.mean(inner, axis=-1, keepdims=True)
        - unit * jnp.mean(inner * unit, axis=-1, keepdims=True)
    )
    return back, back.astype(BF)


def adapter_out(z, r, index, base, sums):
    def inner():
        rows = at(base, CHUNK)
        low = (nt(r.gl[rows, :], r.up_l[index]) * r.gd[index, rows, :]).astype(BF)
        r.inl[rows, :] = low
        for n in range(0, z.width, 256):
            cols = at(n, 256)
            r.sgl[rows, cols] = (r.ssg[rows, cols] + nn(low, r.down_l[index, :, cols])).astype(BF)
        for place in range(2):
            lines = at((2 * index + place) * 8, 8)
            r.acc[lines, :] = sums[place] if base == 0 else r.acc[lines, :] + sums[place]

    yield inner


def second_norm(z, r, base):
    yield from adapt(z, r, 1, base)
    sums = [None, None]
    for row in range(base, base + CHUNK, SUB):

        def unit(row=row):
            rows = at(row, SUB)
            normed, scale = normalize(r.tmp[rows, :])
            r.output[rows, :] = normed * r.norms[2:3, :] + r.norms[3:4, :]
            back, low = norm_back(
                sums, r.cots[rows, :].astype(F32), normed, scale, r.norms[2:3, :]
            )
            r.ssg[rows, :] = back
            r.gl[rows, :] = low

        yield unit
    yield from adapter_out(z, r, 1, base, sums)


def first_out(z, r, base):
    def finish(rows, cols, product):
        r.tmp[rows, cols] = product + r.ssg[rows, cols]

    return big_dot(z, base, r.hid, r.we, nt, finish)


def first_back(z, r, base):
    sums = [None, None]
    for row in range(base, base + CHUNK, SUB):

        def unit(row=row):
            rows = at(row, SUB)
            back, low = norm_back(
                sums, r.tmp[rows, :], r.normed[rows, :], r.scale_s[rows, :], r.norms[0:1, :]
            )
            r.ssg[rows, :] = back
            r.gl[rows, :] = low

        yield unit
    yield from adapter_out(z, r, 0, base, sums)


def collect(z, r, index):
    def down():
        r.grads[index, 0, 0:64, :] = tn(r.inl[...], r.br_l[index])

    def up():
        r.grads[index, 1, 0:72, :] = tn(r.act[index], r.gl[...])[0:72]

    def lines():
        for place in range(2):
            line = jnp.sum(r.acc[at((2 * index + place) * 8, 8), :], axis=0, keepdims=True)
            r.grads[index, 0, 64 + place : 65 + place, :] = line
        r.grads[index, 1, 65:66, 0:64] = jnp.sum(r.inl[...].astype(F32), axis=0, keepdims=True)

    yield down
    yield up
    yield lines


def branch_back(z, r, base):
    for row in range(0, z.width, 256):

        def unit(row=row):
            rows = at(row, 256)
            r.dat[rows, at(base, CHUNK)] = nt(r.wo[rows, :], r.sgl[at(base, CHUNK), :]).astype(BF)

        yield unit


def attend_back(z, r, pair):
    span = z.tok // 2
    cols = at(pair * 128, 128)
    values = r.values[:, cols]
    got = [[], [], []]
    for j in range(2):
        head = pair * 2 + j
        rows = at(pair * 128 + j * 64, 64)
        grad = r.dat[rows, :].astype(F32)
        dot = jnp.sum(grad * r.o_t[rows, :].astype(F32), axis=0, keepdims=True)
        score_grads = []
        value_grads = []
        for kh in range(2):
            weight = r.fac[head, kh : kh + 1, :]
            scaled = (grad * weight).astype(BF)
            pieces = [scaled, jnp.zeros((64, z.tok), BF)]
            spread = jnp.concatenate(pieces if j == 0 else pieces[::-1], axis=0)
            back = nn(values[kh * span : (kh + 1) * span], spread)
            exps = r.ex[head, at(kh * span, span), :]
            score_grads.append((exps.astype(F32) * (back - dot * weight)).astype(BF))
            value_grads.append(nt(scaled, exps))
        scores = jnp.concatenate(score_grads, axis=0)
        got[0].append((nn(r.k_t[rows, :], scores) * (HEAD_DIM ** -0.5)).astype(BF))
        got[1].append(nt(r.q_t[rows, :], scores).astype(BF))
        got[2].append(jnp.concatenate(value_grads, axis=1).astype(BF))
    pairs_half = z.half // 128
    side = lax.div(pair, pairs_half)
    offset = side * 3 * z.half + lax.rem(pair, pairs_half) * 128
    for c in range(3):
        r.dqkv[:, at(offset + c * z.half, 128)] = jnp.concatenate(got[c], axis=0).T


def input_back(z, r, base):
    rows = at(base, CHUNK)
    r.input_grad[rows, :] = r.ssg[rows, :] + nt(r.dqkv[rows, 0 : 6 * z.half], r.w3[...])


def share(r):
    r.dqkv, r.dat, r.sgl, r.gl, r.ssg = r.slope, r.v_t, r.first_l, r.att, r.first_f


def layer_kernel(z, *refs):
    names = [name for name, _ in INPUTS] + ["output", "input_grad", "sums"]
    names += [f"held{index}" for index in range(15)]
    names += [name for name, _ in SCRATCH] + [name for name, _ in SEMAPHORES] + ["lengths"]
    r = types.SimpleNamespace(**dict(zip(names, refs, strict=True)))
    share(r)
    r.down_bias, r.up_bias, r.norms = r.held3, r.held9, r.held12
    tok, width, half, ff_half, n_dp, piece = z.tok, z.width, z.half, z.ff_half, z.n_dp, z.piece
    wide = 3 * half
    dp = lax.axis_index("dp")
    mp = lax.axis_index("mp")
    mate = (dp, 1 - mp)

    def load(src, dst, index):
        copy = pltpu.make_async_copy(src, dst, r.load_sem.at[index])
        copy.start()
        return copy

    load_x = load(r.tokens, r.xs, 0)
    load_w3 = [load(r.triple.at[c], r.w3.at[:, at(c * half, half)], 1 + c) for c in range(3)]

    load_tiny = [
        load(r.lengths_hbm, r.lengths, 25),
        load(r.qv_hbm, r.qv_bias, 26),
        load(r.expand_b_hbm, r.expand_bias, 27),
        load(r.branch_hbm, r.branch_bias, 28),
    ]
    barrier = pltpu.get_barrier_semaphore()
    ready, go = r.meet.at[0], r.meet.at[1]

    @pl.when(mp == 0)
    def call():
        pl.semaphore_signal(barrier, inc=1, device_id=mate, device_id_type=MESH)

    @pl.when(mp == 1)
    def answer():
        pl.semaphore_wait(barrier, 1)
        pl.semaphore_signal(ready, inc=1, device_id=mate, device_id_type=MESH)

    @pl.when(mp == 0)
    def hear():
        pl.semaphore_wait(ready, 1)

    def push(src, dst, index):
        copy = pltpu.make_async_remote_copy(
            src_ref=src,
            dst_ref=dst,
            send_sem=r.far_send.at[index],
            recv_sem=r.far_recv.at[index],
            device_id=mate,
            device_id_type=MESH,
        )
        copy.start()
        return copy

    far_w3 = [
        push(r.triple.at[c], r.w3.at[:, at(wide + c * half, half)], 1 + c) for c in range(3)
    ]

    @pl.when(mp == 0)
    def greet_all():
        def greet(step, carry):
            peer = lax.rem(dp + step, n_dp)
            pl.semaphore_signal(barrier, inc=1, device_id=(peer, mp), device_id_type=MESH)
            return carry

        lax.fori_loop(1, n_dp, greet, 0)

    for copy in load_tiny:
        copy.wait()

    r.bias_own[...] = jnp.zeros_like(r.bias_own)
    r.bias_own[0:2, 0:half] = r.qv_bias[...].astype(F32)
    r.bias_own[2:3, :] = r.expand_bias[...].astype(F32).reshape(1, ff_half)

    ends = []
    total = jnp.int32(0)
    for slot in range(SLOTS - 1):
        total = total + jnp.where(mp == 0, r.lengths[0, slot], r.lengths[1, slot])
        ends.append(total)

    def gather_all():
        @pl.when(mp == 0)
        def first_core():
            pl.semaphore_wait(barrier, n_dp - 1)
            pl.semaphore_signal(go, inc=1, device_id=mate, device_id_type=MESH)

        @pl.when(mp == 1)
        def second_core():
            pl.semaphore_wait(go, 1)

    far_bias = push(r.bias_own, r.bias_far, 0)
    set_masks(z, r, ends)
    r.grads[...] = jnp.zeros_like(r.grads)
    marker = lax.broadcasted_iota(jnp.int32, (tok, 128), 1) == 64
    for index in range(2):
        r.act[index] = jnp.where(marker, 1.0, 0.0).astype(BF)
    load_x.wait()
    for copy in load_w3:
        copy.wait()
    load_down = load(r.param0, r.held0, 4)
    load_up = load(r.param6, r.held6, 5)
    load_small = [
        load(getattr(r, f"param{index}"), getattr(r, f"held{index}"), 10 + index)
        for index in (3, 9, 12)
    ]
    load_wo = load(r.out_w, r.wo.at[at(0, half), :], 6)
    load_we = load(r.expand, r.we.at[:, at(0, ff_half)], 7)
    load_ws = load(r.shrink, r.ws.at[at(0, ff_half), :], 8)
    load_cot = load(r.cot, r.cots, 9)
    weave(project(z, r, 0))
    far_wo = push(r.out_w, r.wo.at[at(half, half), :], 4)
    far_we = push(r.expand, r.we.at[:, at(ff_half, ff_half)], 5)
    weave(attend(z, r, 0))
    far_ws = push(r.shrink, r.ws.at[at(ff_half, ff_half), :], 6)
    far_bias.wait()
    for copy in far_w3:
        copy.wait()
    weave(project(z, r, 1))
    weave(attend(z, r, 1))

    load_down.wait()
    load_up.wait()
    r.down_l[...] = r.held0[...].astype(BF)
    r.up_l[...] = r.held6[...].astype(BF)
    held = [
        load(getattr(r, f"param{index}"), getattr(r, f"held{index}"), 10 + index)
        for index in range(15)
        if index not in (0, 3, 6, 9, 12)
    ]
    for copy in load_small:
        copy.wait()
    load_wo.wait()
    far_wo.wait()
    load_we.wait()

    def core_copy(b):
        return pltpu.make_async_remote_copy(
            src_ref=r.grads.at[b, 1 - mp],
            dst_ref=r.c_recv.at[b],
            send_sem=r.core_send.at[2 * b],
            recv_sem=r.core_recv.at[2 * b],
            device_id=mate,
            device_id_type=MESH,
        )

    def ring_start(b, stage):
        def body(step, carry):
            peer = lax.rem(dp + step, n_dp)
            if stage == 0:
                src, dst = r.rs_buf.at[b, peer], r.rs_recv.at[b, step - 1]
            else:
                src, dst = r.ag_buf.at[b, dp], r.ag_buf.at[b, dp]
            pltpu.make_async_remote_copy(
                src_ref=src,
                dst_ref=dst,
                send_sem=r.ring_send.at[2 * b + stage],
                recv_sem=r.ring_recv.at[2 * b + stage],
                device_id=(peer, mp),
                device_id_type=MESH,
            ).start()
            return carry

        lax.fori_loop(1, n_dp, body, 0)

    def ring_wait(b, stage):
        block = r.rs_recv.at[b]
        pltpu.make_async_copy(block, block, r.ring_send.at[2 * b + stage]).wait()
        pltpu.make_async_copy(block, block, r.ring_recv.at[2 * b + stage]).wait()

    def last_copy(b):
        return pltpu.make_async_remote_copy(
            src_ref=r.ag_buf.at[b],
            dst_ref=r.ag_far.at[b],
            send_sem=r.core_send.at[2 * b + 1],
            recv_sem=r.core_recv.at[2 * b + 1],
            device_id=mate,
            device_id_type=MESH,
        )

    def reduce_one(b):
        core_copy(b).start()

    def reduce_two(b):
        core_copy(b).wait()
        mine = (r.grads[b, mp] + r.c_recv[b]).astype(BF)
        blocks = jnp.concatenate(
            [mine[:, c * 128 : (c + 1) * 128] for c in range(width // 128)], axis=0
        )
        spare = n_dp * piece - blocks.shape[0]
        if spare:
            blocks = jnp.concatenate([blocks, jnp.zeros((spare, 128), BF)], axis=0)
        r.rs_buf[b] = blocks.reshape(n_dp, piece, 128)
        ring_start(b, 0)

    def reduce_three(b):
        ring_wait(b, 0)
        total = jnp.sum(r.rs_recv[b].astype(F32), axis=0) + r.rs_buf[b, dp].astype(F32)
        r.ag_buf[b, dp] = total.astype(BF)
        ring_start(b, 1)

    def reduce_four(b):
        ring_wait(b, 1)
        last_copy(b).start()

    def reduce_five(b):
        last_copy(b).wait()

    late = CHUNK
    att = r.att
    weave(branch_out(z, r, 0, 0, att, r.wo, r.xs))
    weave(branch_out(z, r, 0, late, att, r.wo, r.xs), first_norm(z, r, 0))
    weave(expand(z, r, 0, 0), first_norm(z, r, late))
    weave(expand(z, r, 0, late))
    load_ws.wait()
    weave(shrink_own(z, r, 0))
    weave(shrink_own(z, r, late))
    gather_all()
    load_cot.wait()
    far_we.wait()
    weave(expand(z, r, 1, 0))
    far_ws.wait()
    weave(shrink_far(z, r, 0))
    weave([*expand(z, r, 1, late), *shrink_far(z, r, late)], second_norm(z, r, 0))
    weave(unshrink(z, r, 0), second_norm(z, r, late))
    weave(unshrink(z, r, late), collect(z, r, 1))
    reduce_one(1)
    weave(first_out(z, r, 0))
    weave(first_out(z, r, late), first_back(z, r, 0))
    reduce_two(1)
    weave(branch_back(z, r, 0), first_back(z, r, late))
    weave(collect(z, r, 0))
    reduce_one(0)
    weave(branch_back(z, r, late))

    def back(pair, carry):
        attend_back(z, r, pair)
        return carry

    pairs = width // 128
    middle = pairs // 2
    lax.fori_loop(0, 1, back, 0)
    reduce_two(0)
    lax.fori_loop(1, middle, back, 0)
    reduce_three(1)
    lax.fori_loop(middle, pairs - 1, back, 0)
    reduce_three(0)
    lax.fori_loop(pairs - 1, pairs, back, 0)
    for base in range(0, tok, CHUNK):
        input_back(z, r, base)
    reduce_four(1)
    for copy in held:
        copy.wait()
    reduce_five(1)
    reduce_four(0)
    for b in range(2):
        r.sums[b, mp] = r.ag_buf[b]
    r.sums[1, 1 - mp] = r.ag_far[1]
    reduce_five(0)
    r.sums[0, 1 - mp] = r.ag_far[0]


def update_kernel(blocks, step, output_src, input_grad_src, sums, *refs):
    params, rest = refs[:15], refs[15:]
    output, input_grad, norm_out = rest[:3]
    targets, news, sem = rest[3:18], rest[18:33], rest[33]
    stores = []

    def store(src, dst):
        copy = pltpu.make_async_copy(src, dst, sem.at[len(stores)])
        copy.start()
        stores.append(copy)

    store(output_src, output)
    store(input_grad_src, input_grad)
    squares = jnp.zeros((8, 128), F32)
    for b in range(2):
        for side in range(2):
            part = sums[b, side].astype(F32)
            squares = squares + fold_rows(part * part)
    squares = jnp.sum(jnp.sum(squares, axis=0, keepdims=True), axis=1, keepdims=True)
    grad_norm = jnp.sqrt(squares)
    norm_out[...] = grad_norm
    clip = jnp.minimum(1.0, CLIP_LIMIT / (grad_norm + 1e-06))
    count = jnp.full((1, 1), step[0], jnp.int32).astype(F32)
    fix_one = 1.0 - jnp.exp2(count * jnp.log2(jnp.full((1, 1), 0.9, F32)))
    fix_two = 1.0 - jnp.exp2(count * jnp.log2(jnp.full((1, 1), 0.999, F32)))
    over_one = 1.0 / fix_one
    over_two = 1.0 / fix_two

    def update(index, where, grad):
        weight, first, second = (params[3 * index + n][where] for n in range(3))
        rate, decay = RATES[index]
        clipped = grad * clip
        first_new = 0.9 * first + 0.1 * clipped
        second_new = 0.999 * second + 0.001 * clipped * clipped
        move = first_new * over_one / (jnp.sqrt(second_new * over_two) + 1e-08)
        if decay:
            move = move + decay * weight
        news[3 * index][where] = weight - rate * move
        news[3 * index + 1][where] = first_new
        news[3 * index + 2][where] = second_new

    lines = {}
    for side in range(2):
        for b in range(2):
            tops = []
            for c in range(blocks):
                block = sums[b, side, pl.ds(c * PART, PART), :].astype(F32)
                update(2 * side, (b, slice(None), slice(c * 128, (c + 1) * 128)), block[0:64])
                tops.append(block[64:72])
            lines[b, side] = jnp.concatenate(tops, axis=1)
        for n in range(3):
            store(news[6 * side + n], targets[6 * side + n])
    for b in range(2):
        update(4, (slice(2 * b, 2 * b + 2), slice(None)), lines[b, 0][0:2])
        update(3, (slice(b, b + 1), slice(None)), lines[b, 1][0:1])
        update(1, (slice(b, b + 1), slice(None)), lines[b, 1][1:2, 0:64])
    for index in (3, 4, 5, 9, 10, 11, 12, 13, 14):
        store(news[index], targets[index])
    for copy in stores:
        copy.wait()


def per_device(
    n_dp,
    tokens,
    lengths,
    cotangent,
    triple_weight,
    query_value_bias,
    output_weight,
    branch_bias,
    expand_weight,
    expand_bias,
    shrink_weight,
    adapter_down,
    down_bias,
    adapter_up,
    up_bias,
    norm_params,
    adapter_down_first,
    adapter_down_second,
    down_bias_first,
    down_bias_second,
    adapter_up_first,
    adapter_up_second,
    up_bias_first,
    up_bias_second,
    norm_params_first,
    norm_params_second,
    step,
):
    tok, width = tokens.shape
    half = triple_weight.shape[2]
    ff_half = expand_weight.shape[1]
    ff = 2 * ff_half
    heads = 2 * half // HEAD_DIM
    blocks = width // 128
    piece = -(-(PART * blocks) // (16 * n_dp)) * 16
    z = types.SimpleNamespace(
        tok=tok,
        width=width,
        half=half,
        ff_half=ff_half,
        ff=ff,
        heads=heads,
        n_dp=n_dp,
        piece=piece,
    )
    flip = lambda v: jnp.swapaxes(v, 1, 2)
    spaces = {
        "s": pl.BlockSpec(memory_space=pltpu.SMEM),
        "v": pl.BlockSpec(memory_space=pltpu.VMEM),
        "h": pl.BlockSpec(memory_space=pltpu.HBM),
    }
    vmem, smem, hbm = spaces["v"], spaces["s"], spaces["h"]
    params = (
        flip(adapter_down),
        flip(adapter_down_first),
        flip(adapter_down_second),
        down_bias,
        down_bias_first,
        down_bias_second,
        adapter_up,
        adapter_up_first,
        adapter_up_second,
        up_bias,
        up_bias_first,
        up_bias_second,
        norm_params,
        norm_params_first,
        norm_params_second,
    )
    operands = (
        lengths,
        query_value_bias,
        branch_bias,
        expand_bias,
        tokens,
        cotangent,
        jnp.transpose(triple_weight, (1, 0, 2)),
        output_weight,
        expand_weight,
        shrink_weight,
        *params,
    )
    output, input_grad, sums, *held = pl.pallas_call(
        functools.partial(layer_kernel, z),
        out_shape=(
            pltpu.VMEM((tok, width), F32),
            pltpu.VMEM((tok, width), F32),
            pltpu.VMEM((2, 2, n_dp, piece, 128), BF),
            *(pltpu.VMEM(p.shape, F32) for p in params),
        ),
        in_specs=[spaces[space] for _, space in INPUTS],
        out_specs=(vmem,) * 18,
        scratch_shapes=[pltpu.VMEM(*make(z)) for _, make in SCRATCH]
        + [
            pltpu.SemaphoreType.DMA((count,)) if count else pltpu.SemaphoreType.REGULAR((2,))
            for _, count in SEMAPHORES
        ]
        + [pltpu.SMEM(lengths.shape, jnp.int32)],
        compiler_params=pltpu.CompilerParams(
            collective_id=0, has_side_effects=True, vmem_limit_bytes=56 * 2**20
        ),
    )(*operands)
    sums = sums.reshape(2, 2, n_dp * piece, 128)
    results = pl.pallas_call(
        functools.partial(update_kernel, blocks),
        out_shape=(
            jax.ShapeDtypeStruct((tok, width), F32),
            jax.ShapeDtypeStruct((tok, width), F32),
            jax.ShapeDtypeStruct((1, 1), F32),
            *(jax.ShapeDtypeStruct(p.shape, F32) for p in params),
        ),
        in_specs=[smem] + [vmem] * 18,
        out_specs=(hbm, hbm, vmem) + (hbm,) * 15,
        scratch_shapes=[pltpu.VMEM(p.shape, F32) for p in params]
        + [pltpu.SemaphoreType.DMA((17,))],
        compiler_params=pltpu.CompilerParams(vmem_limit_bytes=16 * 2**20),
    )(step, output, input_grad, sums, *held)
    news = list(results[3:])
    for index in range(3):
        news[index] = flip(news[index])
    return (results[0], results[1], results[2].reshape(1), *news)


def solution(mesh):
    split = P(("dp", "mp"), None)
    in_specs = (
        split,
        P("dp", None),
        split,
        P(None, None, "mp"),
        P(None, "mp"),
        P("mp", None),
        P(),
        P(None, "mp"),
        P("mp"),
        P("mp", None),
    ) + (P(),) * 16
    out_specs = (split, split) + (P(),) * 16
    return jax.shard_map(
        functools.partial(per_device, mesh.shape["dp"]),
        mesh=mesh,
        in_specs=in_specs,
        out_specs=out_specs,
        check_vma=False,
    )
```

```python
import functools
import types

import jax
import jax.numpy as jnp
from jax import lax
from jax.experimental import pallas as pl
from jax.experimental.pallas import tpu as pltpu
from jax.sharding import PartitionSpec as P

HEAD_DIM = 64
SLOTS = 8
EPSILON = 1e-12
CLIP_LIMIT = 1.0
LOG2E = 1.4426950408889634
HALF_ROOT = 0.7071067811865476
DENSITY = 0.3989422804014327
NEGATIVE = -1e30
RATES = ((0.03, 0.01), (0.1, 0.0), (0.1, 0.01), (0.1, 0.0), (0.2, 0.0))
PART = 80
MESH = pl.DeviceIdType.MESH
BF = jnp.bfloat16
F32 = jnp.float32


def nn(a, b):
    return lax.dot_general(a, b, (((1,), (0,)), ((), ())), preferred_element_type=F32)


def nt(a, b):
    return lax.dot_general(a, b, (((1,), (1,)), ((), ())), preferred_element_type=F32)


def tn(a, b):
    return lax.dot_general(a, b, (((0,), (0,)), ((), ())), preferred_element_type=F32)


def at(start, size, step=None):
    if isinstance(start, int):
        return pl.ds(start, size)
    return pl.ds(pl.multiple_of(start, step or size), size)


def gelu_parts(value):
    mass = 0.5 + 0.5 * lax.erf(value * HALF_ROOT)
    slope = mass + value * (jnp.exp2(value * value * (-0.5 * LOG2E)) * DENSITY)
    return value * mass, slope


def fold_rows(value):
    rows, width = value.shape
    return jnp.sum(value.reshape(rows // 8, 8, width), axis=0)


SCRATCH = (
    ("qv_bias", lambda z: ((2, z.half), BF)),
    ("branch_bias", lambda z: ((2, z.width), BF)),
    ("expand_bias", lambda z: ((z.ff_half,), BF)),
    ("xs", lambda z: ((z.tok, z.width), BF)),
    ("cots", lambda z: ((z.tok, z.width), BF)),
    ("w3", lambda z: ((z.width, 6 * z.half), BF)),
    ("wo", lambda z: ((2 * z.half, z.width), BF)),
    ("we", lambda z: ((z.width, z.ff), BF)),
    ("ws", lambda z: ((z.ff, z.width), BF)),
    ("down_l", lambda z: ((2, 64, z.width), BF)),
    ("up_l", lambda z: ((2, 64, z.width), BF)),
    ("bias_own", lambda z: ((8, z.ff_half), F32)),
    ("bias_far", lambda z: ((8, z.ff_half), F32)),
    ("keys", lambda z: ((z.tok, z.width), BF)),
    ("values", lambda z: ((z.tok, z.width), BF)),
    ("q_t", lambda z: ((z.width, z.tok), BF)),
    ("k_t", lambda z: ((z.width, z.tok), BF)),
    ("v_t", lambda z: ((z.width, z.tok), BF)),
    ("hot", lambda z: ((z.tok, 128), BF)),
    ("qa", lambda z: ((4 * 256, z.tok), BF)),
    ("ex", lambda z: ((z.heads, z.tok, z.tok), BF)),
    ("fac", lambda z: ((z.heads, 8, z.tok), F32)),
    ("o_t", lambda z: ((z.width, z.tok), BF)),
    ("att", lambda z: ((z.tok, z.width), BF)),
    ("br_l", lambda z: ((2, z.tok, z.width), BF)),
    ("act", lambda z: ((2, z.tok, 128), BF)),
    ("gd", lambda z: ((2, z.tok, 64), F32)),
    ("inl", lambda z: ((z.tok, 64), BF)),
    ("normed", lambda z: ((z.tok, z.width), F32)),
    ("scale_s", lambda z: ((z.tok, 1), F32)),
    ("first_f", lambda z: ((z.tok, z.width), F32)),
    ("first_l", lambda z: ((z.tok, z.width), BF)),
    ("hid", lambda z: ((z.tok, z.ff), BF)),
    ("slope", lambda z: ((z.tok, z.ff), BF)),
    ("tmp", lambda z: ((z.tok, z.width), F32)),
    ("grads", lambda z: ((2, 2, PART, z.width), F32)),
    ("acc", lambda z: ((48, z.width), F32)),
    ("c_recv", lambda z: ((2, PART, z.width), F32)),
    ("rs_buf", lambda z: ((2, z.n_dp, z.piece, 128), BF)),
    ("rs_recv", lambda z: ((2, z.n_dp - 1, z.piece, 128), BF)),
    ("ag_buf", lambda z: ((2, z.n_dp, z.piece, 128), BF)),
    ("ag_far", lambda z: ((2, z.n_dp, z.piece, 128), BF)),
)
SEMAPHORES = (
    ("load_sem", 29),
    ("meet", 0),
    ("far_send", 7),
    ("far_recv", 7),
    ("core_send", 4),
    ("core_recv", 4),
    ("ring_send", 4),
    ("ring_recv", 4),
)
INPUTS = (
    ("lengths_hbm", "h"),
    ("qv_hbm", "h"),
    ("branch_hbm", "h"),
    ("expand_b_hbm", "h"),
    ("tokens", "h"),
    ("cot", "h"),
    ("triple", "h"),
    ("out_w", "h"),
    ("expand", "h"),
    ("shrink", "h"),
    *((f"param{index}", "h") for index in range(15)),
)
CHUNK = 256
SUB = 32


def weave(*works):
    queues = [[list(work), 0] for work in works]
    most = max(len(queue[0]) for queue in queues)
    for tick in range(most):
        for queue in queues:
            units, done = queue
            goal = -(-len(units) * (tick + 1) // most)
            for unit in units[done:goal]:
                unit()
            queue[1] = max(done, goal)


def normalize(v):
    center = v - jnp.mean(v, axis=-1, keepdims=True)
    scale = lax.rsqrt(jnp.mean(center * center, axis=-1, keepdims=True) + EPSILON)
    return center * scale, scale


def set_masks(z, r, ends):
    def marks(shape, axis):
        place = lax.broadcasted_iota(jnp.int32, shape, axis)
        found = jnp.zeros(shape, jnp.int32)
        for end in ends:
            found = found + (place >= end).astype(jnp.int32)
        return found

    tok = z.tok
    r.hot[...] = jnp.where(
        marks((tok, 128), 0) == lax.broadcasted_iota(jnp.int32, (tok, 128), 1), 1.0, 0.0
    ).astype(BF)
    shut = jnp.where(
        marks((128, tok), 1) == lax.broadcasted_iota(jnp.int32, (128, tok), 0), 0.0, NEGATIVE
    ).astype(BF)
    for slot in range(4):
        r.qa[at(slot * 256, 128), :] = jnp.zeros((128, tok), BF)
        r.qa[at(slot * 256 + 128, 128), :] = shut


def project(z, r, side):
    bias = (r.bias_own, r.bias_far)[side]
    base = side * 3 * z.half
    for n in range(0, 3 * z.half, 256):

        def unit(n=n):
            size = min(256, 3 * z.half - n)
            mixed = nn(r.xs[...], r.w3[:, at(base + n, size)])
            for start in range(n, n + size, 128):
                c, col = start // z.half, start % z.half
                part = mixed[:, start - n : start - n + 128]
                if c != 1:
                    part = part + bias[c // 2 : c // 2 + 1, at(col, 128)]
                low = part.astype(BF)
                place = at(side * z.half + col, 128)
                if c == 0:
                    r.q_t[place, :] = (low.astype(F32) * (HEAD_DIM ** -0.5)).astype(BF).T
                if c == 1:
                    r.keys[:, place] = low
                    r.k_t[place, :] = low.T
                if c == 2:
                    r.values[:, place] = low
                    r.v_t[place, :] = low.T

        yield unit


def attend(z, r, side):
    span = z.tok // 2
    first = side * z.half // HEAD_DIM
    count = z.half // HEAD_DIM
    ones = jnp.ones((16, z.tok), BF)
    kept = {}

    def score(head, kh, c):
        slot = head % 4
        if kh == 0 and c == 0:
            r.qa[at(slot * 256 + head % 2 * 64, 64), :] = r.q_t[at(head * 64, 64), :]
        part = at(kh * span, span)
        keys = jnp.concatenate([r.keys[part, at(head // 2 * 128, 128)], r.hot[part, :]], axis=1)
        return nn(keys, r.qa[at(slot * 256, 256), at(c * span, span)])

    def exponents(head, kh, c, s):
        top = jnp.max(s, axis=0, keepdims=True) * LOG2E
        r.ex[head, at(kh * span, span), at(c * span, span)] = jnp.exp2(s * LOG2E - top).astype(BF)
        kept[head, kh, c] = top

    def gather(head):
        rows = at(head * 64, 64)
        values = jnp.concatenate([r.v_t[rows, :], ones], axis=0)
        parts = [
            nn(values[:, kh * span : (kh + 1) * span], r.ex[head, at(kh * span, span), :])
            for kh in range(2)
        ]
        peaks = [
            jnp.concatenate([kept.pop((head, kh, c)) for c in range(2)], axis=1) for kh in range(2)
        ]
        peak = jnp.maximum(peaks[0], peaks[1])
        weights = [jnp.exp2(p - peak) for p in peaks]
        inverse = 1.0 / (parts[0][64:65] * weights[0] + parts[1][64:65] * weights[1])
        weights = [w * inverse for w in weights]
        r.fac[head, 0:1, :] = weights[0]
        r.fac[head, 1:2, :] = weights[1]
        r.o_t[rows, :] = (parts[0][:64] * weights[0] + parts[1][:64] * weights[1]).astype(BF)
        if head % 2:
            cols = at(head // 2 * 128, 128)
            r.att[:, cols] = r.o_t[cols, :].T

    units = [(head, kh, c) for head in range(first, first + count) for kh in range(2) for c in range(2)]
    ahead = []
    yield lambda: ahead.append(score(*units[0]))
    for index, unit in enumerate(units):

        def step(index=index, unit=unit):
            s = ahead.pop()
            if index + 1 < len(units):
                ahead.append(score(*units[index + 1]))
            exponents(*unit, s)
            if unit[1:] == (1, 1) and unit[0] > first:
                gather(unit[0] - 1)

        yield step
    yield lambda: gather(first + count - 1)


def big_dot(z, base, left, right, form, finish):
    rows = at(base, CHUNK)
    for n in range(0, z.width, 256):

        def unit(n=n):
            cols = at(n, 256)
            weights = right[:, cols] if form is nn else right[cols, :]
            finish(rows, cols, form(left[rows, :], weights))

        yield unit


def branch_out(z, r, index, base, left, right, before):
    def finish(rows, cols, product):
        value = product + r.branch_bias[index : index + 1, cols].astype(F32)
        r.br_l[index, rows, cols] = value.astype(BF)
        r.tmp[rows, cols] = value + before[rows, cols].astype(F32)

    return big_dot(z, base, left, right, nn, finish)


def shrink_own(z, r, base):
    rows = at(base, CHUNK)
    for n in range(0, z.width, 256):

        def unit(n=n):
            own = at(0, z.ff_half)
            r.tmp[rows, at(n, 256)] = nn(r.hid[rows, own], r.ws[own, at(n, 256)])

        yield unit


def shrink_far(z, r, base):
    def finish(rows, cols, product):
        value = product + r.tmp[rows, cols] + r.branch_bias[1:2, cols].astype(F32)
        r.br_l[1, rows, cols] = value.astype(BF)
        r.tmp[rows, cols] = value + r.first_f[rows, cols]

    far = at(z.ff_half, z.ff_half)
    return big_dot(z, base, r.hid.at[:, far], r.ws.at[far, :], nn, finish)


def adapt(z, r, index, base):
    def inner():
        rows = at(base, CHUNK)
        value, grade = gelu_parts(
            nt(r.br_l[index, rows, :], r.down_l[index]) + r.down_bias[index : index + 1, :]
        )
        low = value.astype(BF)
        r.act[index, rows, 0:64] = low
        r.gd[index, rows, :] = grade
        for n in range(0, z.width, 256):
            cols = at(n, 256)
            r.tmp[rows, cols] += nn(low, r.up_l[index, :, cols]) + r.up_bias[index : index + 1, cols]

    yield inner


def first_norm(z, r, base):
    yield from adapt(z, r, 0, base)
    for row in range(base, base + CHUNK, SUB):

        def unit(row=row):
            rows = at(row, SUB)
            normed, scale = normalize(r.tmp[rows, :])
            r.normed[rows, :] = normed
            r.scale_s[rows, :] = scale
            first = normed * r.norms[0:1, :] + r.norms[1:2, :]
            r.first_f[rows, :] = first
            r.first_l[rows, :] = first.astype(BF)

        yield unit


def expand(z, r, side, base):
    bias = (r.bias_own, r.bias_far)[side]
    rows = at(base, CHUNK)
    for j in range(0, z.ff_half, 256):

        def unit(j=j):
            cols = at(side * z.ff_half + j, 256)
            before = nn(r.first_l[rows, :], r.we[:, cols]) + bias[2:3, at(j, 256)]
            value, grade = gelu_parts(before)
            r.hid[rows, cols] = value.astype(BF)
            r.slope[rows, cols] = grade.astype(BF)

        yield unit


def unshrink(z, r, base):
    rows = at(base, CHUNK)
    for j in range(0, z.ff, 256):

        def unit(j=j):
            cols = at(j, 256)
            grad = nt(r.sgl[rows, :], r.ws[cols, :])
            r.hid[rows, cols] = (grad * r.slope[rows, cols].astype(F32)).astype(BF)

        yield unit


def norm_back(sums, grad, unit, scale, gain):
    for place, part in enumerate((fold_rows(grad * unit), fold_rows(grad))):
        sums[place] = part if sums[place] is None else sums[place] + part
    inner = grad * gain
    back = scale * (
        inner
        - jnp.mean(inner, axis=-1, keepdims=True)
        - unit * jnp.mean(inner * unit, axis=-1, keepdims=True)
    )
    return back, back.astype(BF)


def adapter_out(z, r, index, base, sums):
    def inner():
        rows = at(base, CHUNK)
        low = (nt(r.gl[rows, :], r.up_l[index]) * r.gd[index, rows, :]).astype(BF)
        r.inl[rows, :] = low
        for n in range(0, z.width, 256):
            cols = at(n, 256)
            r.sgl[rows, cols] = (r.ssg[rows, cols] + nn(low, r.down_l[index, :, cols])).astype(BF)
        for place in range(2):
            lines = at((2 * index + place) * 8, 8)
            r.acc[lines, :] = sums[place] if base == 0 else r.acc[lines, :] + sums[place]

    yield inner


def second_norm(z, r, base):
    yield from adapt(z, r, 1, base)
    sums = [None, None]
    for row in range(base, base + CHUNK, SUB):

        def unit(row=row):
            rows = at(row, SUB)
            normed, scale = normalize(r.tmp[rows, :])
            r.output[rows, :] = normed * r.norms[2:3, :] + r.norms[3:4, :]
            back, low = norm_back(
                sums, r.cots[rows, :].astype(F32), normed, scale, r.norms[2:3, :]
            )
            r.ssg[rows, :] = back
            r.gl[rows, :] = low

        yield unit
    yield from adapter_out(z, r, 1, base, sums)


def first_out(z, r, base):
    def finish(rows, cols, product):
        r.tmp[rows, cols] = product + r.ssg[rows, cols]

    return big_dot(z, base, r.hid, r.we, nt, finish)


def first_back(z, r, base):
    sums = [None, None]
    for row in range(base, base + CHUNK, SUB):

        def unit(row=row):
            rows = at(row, SUB)
            back, low = norm_back(
                sums, r.tmp[rows, :], r.normed[rows, :], r.scale_s[rows, :], r.norms[0:1, :]
            )
            r.ssg[rows, :] = back
            r.gl[rows, :] = low

        yield unit
    yield from adapter_out(z, r, 0, base, sums)


def collect(z, r, index):
    def down():
        r.grads[index, 0, 0:64, :] = tn(r.inl[...], r.br_l[index])

    def up():
        r.grads[index, 1, 0:72, :] = tn(r.act[index], r.gl[...])[0:72]

    def lines():
        for place in range(2):
            line = jnp.sum(r.acc[at((2 * index + place) * 8, 8), :], axis=0, keepdims=True)
            r.grads[index, 0, 64 + place : 65 + place, :] = line
        r.grads[index, 1, 65:66, 0:64] = jnp.sum(r.inl[...].astype(F32), axis=0, keepdims=True)

    yield down
    yield up
    yield lines


def branch_back(z, r, base):
    for row in range(0, z.width, 256):

        def unit(row=row):
            rows = at(row, 256)
            r.dat[rows, at(base, CHUNK)] = nt(r.wo[rows, :], r.sgl[at(base, CHUNK), :]).astype(BF)

        yield unit


def attend_back(z, r, pair):
    span = z.tok // 2
    cols = at(pair * 128, 128)
    values = r.values[:, cols]
    got = [[], [], []]
    for j in range(2):
        head = pair * 2 + j
        rows = at(pair * 128 + j * 64, 64)
        grad = r.dat[rows, :].astype(F32)
        dot = jnp.sum(grad * r.o_t[rows, :].astype(F32), axis=0, keepdims=True)
        score_grads = []
        value_grads = []
        for kh in range(2):
            weight = r.fac[head, kh : kh + 1, :]
            scaled = (grad * weight).astype(BF)
            pieces = [scaled, jnp.zeros((64, z.tok), BF)]
            spread = jnp.concatenate(pieces if j == 0 else pieces[::-1], axis=0)
            back = nn(values[kh * span : (kh + 1) * span], spread)
            exps = r.ex[head, at(kh * span, span), :]
            score_grads.append((exps.astype(F32) * (back - dot * weight)).astype(BF))
            value_grads.append(nt(scaled, exps))
        scores = jnp.concatenate(score_grads, axis=0)
        got[0].append((nn(r.k_t[rows, :], scores) * (HEAD_DIM ** -0.5)).astype(BF))
        got[1].append(nt(r.q_t[rows, :], scores).astype(BF))
        got[2].append(jnp.concatenate(value_grads, axis=1).astype(BF))
    pairs_half = z.half // 128
    side = lax.div(pair, pairs_half)
    offset = side * 3 * z.half + lax.rem(pair, pairs_half) * 128
    for c in range(3):
        r.dqkv[:, at(offset + c * z.half, 128)] = jnp.concatenate(got[c], axis=0).T


def input_back(z, r, base):
    rows = at(base, CHUNK)
    r.input_grad[rows, :] = r.ssg[rows, :] + nt(r.dqkv[rows, 0 : 6 * z.half], r.w3[...])


def share(r):
    r.dqkv, r.dat, r.sgl, r.gl, r.ssg = r.slope, r.v_t, r.first_l, r.att, r.first_f


def layer_kernel(z, *refs):
    names = [name for name, _ in INPUTS] + ["output", "input_grad", "sums"]
    names += [f"held{index}" for index in range(15)]
    names += [name for name, _ in SCRATCH] + [name for name, _ in SEMAPHORES] + ["lengths"]
    r = types.SimpleNamespace(**dict(zip(names, refs, strict=True)))
    share(r)
    r.down_bias, r.up_bias, r.norms = r.held3, r.held9, r.held12
    tok, width, half, ff_half, n_dp, piece = z.tok, z.width, z.half, z.ff_half, z.n_dp, z.piece
    wide = 3 * half
    dp = lax.axis_index("dp")
    mp = lax.axis_index("mp")
    mate = (dp, 1 - mp)

    def load(src, dst, index):
        copy = pltpu.make_async_copy(src, dst, r.load_sem.at[index])
        copy.start()
        return copy

    load_x = load(r.tokens, r.xs, 0)
    load_w3 = [load(r.triple.at[c], r.w3.at[:, at(c * half, half)], 1 + c) for c in range(3)]

    load_tiny = [
        load(r.lengths_hbm, r.lengths, 25),
        load(r.qv_hbm, r.qv_bias, 26),
        load(r.expand_b_hbm, r.expand_bias, 27),
        load(r.branch_hbm, r.branch_bias, 28),
    ]
    barrier = pltpu.get_barrier_semaphore()
    ready, go = r.meet.at[0], r.meet.at[1]

    @pl.when(mp == 0)
    def call():
        pl.semaphore_signal(barrier, inc=1, device_id=mate, device_id_type=MESH)

    @pl.when(mp == 1)
    def answer():
        pl.semaphore_wait(barrier, 1)
        pl.semaphore_signal(ready, inc=1, device_id=mate, device_id_type=MESH)

    @pl.when(mp == 0)
    def hear():
        pl.semaphore_wait(ready, 1)

    def push(src, dst, index):
        copy = pltpu.make_async_remote_copy(
            src_ref=src,
            dst_ref=dst,
            send_sem=r.far_send.at[index],
            recv_sem=r.far_recv.at[index],
            device_id=mate,
            device_id_type=MESH,
        )
        copy.start()
        return copy

    far_w3 = [
        push(r.triple.at[c], r.w3.at[:, at(wide + c * half, half)], 1 + c) for c in range(3)
    ]

    @pl.when(mp == 0)
    def greet_all():
        def greet(step, carry):
            peer = lax.rem(dp + step, n_dp)
            pl.semaphore_signal(barrier, inc=1, device_id=(peer, mp), device_id_type=MESH)
            return carry

        lax.fori_loop(1, n_dp, greet, 0)

    for copy in load_tiny:
        copy.wait()

    r.bias_own[...] = jnp.zeros_like(r.bias_own)
    r.bias_own[0:2, 0:half] = r.qv_bias[...].astype(F32)
    r.bias_own[2:3, :] = r.expand_bias[...].astype(F32).reshape(1, ff_half)

    ends = []
    total = jnp.int32(0)
    for slot in range(SLOTS - 1):
        total = total + jnp.where(mp == 0, r.lengths[0, slot], r.lengths[1, slot])
        ends.append(total)

    def gather_all():
        @pl.when(mp == 0)
        def first_core():
            pl.semaphore_wait(barrier, n_dp - 1)
            pl.semaphore_signal(go, inc=1, device_id=mate, device_id_type=MESH)

        @pl.when(mp == 1)
        def second_core():
            pl.semaphore_wait(go, 1)

    far_bias = push(r.bias_own, r.bias_far, 0)
    set_masks(z, r, ends)
    r.grads[...] = jnp.zeros_like(r.grads)
    marker = lax.broadcasted_iota(jnp.int32, (tok, 128), 1) == 64
    for index in range(2):
        r.act[index] = jnp.where(marker, 1.0, 0.0).astype(BF)
    load_x.wait()
    for copy in load_w3:
        copy.wait()
    load_down = load(r.param0, r.held0, 4)
    load_up = load(r.param6, r.held6, 5)
    load_small = [
        load(getattr(r, f"param{index}"), getattr(r, f"held{index}"), 10 + index)
        for index in (3, 9, 12)
    ]
    load_wo = load(r.out_w, r.wo.at[at(0, half), :], 6)
    load_we = load(r.expand, r.we.at[:, at(0, ff_half)], 7)
    load_ws = load(r.shrink, r.ws.at[at(0, ff_half), :], 8)
    load_cot = load(r.cot, r.cots, 9)
    weave(project(z, r, 0))
    far_wo = push(r.out_w, r.wo.at[at(half, half), :], 4)
    far_we = push(r.expand, r.we.at[:, at(ff_half, ff_half)], 5)
    weave(attend(z, r, 0))
    far_ws = push(r.shrink, r.ws.at[at(ff_half, ff_half), :], 6)
    far_bias.wait()
    for copy in far_w3:
        copy.wait()
    weave(project(z, r, 1))
    weave(attend(z, r, 1))

    load_down.wait()
    load_up.wait()
    r.down_l[...] = r.held0[...].astype(BF)
    r.up_l[...] = r.held6[...].astype(BF)
    held = [
        load(getattr(r, f"param{index}"), getattr(r, f"held{index}"), 10 + index)
        for index in range(15)
        if index not in (0, 3, 6, 9, 12)
    ]
    for copy in load_small:
        copy.wait()
    load_wo.wait()
    far_wo.wait()
    load_we.wait()

    def core_copy(b):
        return pltpu.make_async_remote_copy(
            src_ref=r.grads.at[b, 1 - mp],
            dst_ref=r.c_recv.at[b],
            send_sem=r.core_send.at[2 * b],
            recv_sem=r.core_recv.at[2 * b],
            device_id=mate,
            device_id_type=MESH,
        )

    def ring_start(b, stage):
        def body(step, carry):
            peer = lax.rem(dp + step, n_dp)
            if stage == 0:
                src, dst = r.rs_buf.at[b, peer], r.rs_recv.at[b, step - 1]
            else:
                src, dst = r.ag_buf.at[b, dp], r.ag_buf.at[b, dp]
            pltpu.make_async_remote_copy(
                src_ref=src,
                dst_ref=dst,
                send_sem=r.ring_send.at[2 * b + stage],
                recv_sem=r.ring_recv.at[2 * b + stage],
                device_id=(peer, mp),
                device_id_type=MESH,
            ).start()
            return carry

        if n_dp > 16:
            lax.fori_loop(1, n_dp, body, 0)
        else:
            for step in range(1, n_dp):
                body(step, 0)

    def ring_wait(b, stage):
        block = r.rs_recv.at[b]
        pltpu.make_async_copy(block, block, r.ring_send.at[2 * b + stage]).wait()
        pltpu.make_async_copy(block, block, r.ring_recv.at[2 * b + stage]).wait()

    def last_copy(b):
        return pltpu.make_async_remote_copy(
            src_ref=r.ag_buf.at[b],
            dst_ref=r.ag_far.at[b],
            send_sem=r.core_send.at[2 * b + 1],
            recv_sem=r.core_recv.at[2 * b + 1],
            device_id=mate,
            device_id_type=MESH,
        )

    def reduce_one(b):
        core_copy(b).start()

    def reduce_two(b):
        core_copy(b).wait()
        mine = (r.grads[b, mp] + r.c_recv[b]).astype(BF)
        blocks = jnp.concatenate(
            [mine[:, c * 128 : (c + 1) * 128] for c in range(width // 128)], axis=0
        )
        spare = n_dp * piece - blocks.shape[0]
        if spare:
            blocks = jnp.concatenate([blocks, jnp.zeros((spare, 128), BF)], axis=0)
        r.rs_buf[b] = blocks.reshape(n_dp, piece, 128)
        ring_start(b, 0)

    def reduce_three(b):
        ring_wait(b, 0)
        total = jnp.sum(r.rs_recv[b].astype(F32), axis=0) + r.rs_buf[b, dp].astype(F32)
        r.ag_buf[b, dp] = total.astype(BF)
        ring_start(b, 1)

    def reduce_four(b):
        ring_wait(b, 1)
        last_copy(b).start()

    def reduce_five(b):
        last_copy(b).wait()

    late = CHUNK
    att = r.att
    weave(branch_out(z, r, 0, 0, att, r.wo, r.xs))
    weave(branch_out(z, r, 0, late, att, r.wo, r.xs), first_norm(z, r, 0))
    weave(expand(z, r, 0, 0), first_norm(z, r, late))
    weave(expand(z, r, 0, late))
    load_ws.wait()
    weave(shrink_own(z, r, 0))
    weave(shrink_own(z, r, late))
    gather_all()
    load_cot.wait()
    far_we.wait()
    weave(expand(z, r, 1, 0))
    far_ws.wait()
    weave(shrink_far(z, r, 0))
    weave([*expand(z, r, 1, late), *shrink_far(z, r, late)], second_norm(z, r, 0))
    weave(unshrink(z, r, 0), second_norm(z, r, late))
    weave(unshrink(z, r, late), collect(z, r, 1))
    reduce_one(1)
    weave(first_out(z, r, 0))
    weave(first_out(z, r, late), first_back(z, r, 0))
    reduce_two(1)
    weave(branch_back(z, r, 0), first_back(z, r, late))
    weave(collect(z, r, 0))
    reduce_one(0)
    weave(branch_back(z, r, late))

    def back(pair, carry):
        attend_back(z, r, pair)
        return carry

    pairs = width // 128
    middle = pairs // 2
    lax.fori_loop(0, 1, back, 0)
    reduce_two(0)
    lax.fori_loop(1, middle, back, 0)
    reduce_three(1)
    lax.fori_loop(middle, pairs - 1, back, 0)
    reduce_three(0)
    lax.fori_loop(pairs - 1, pairs, back, 0)
    for base in range(0, tok, CHUNK):
        input_back(z, r, base)
    reduce_four(1)
    for copy in held:
        copy.wait()
    reduce_five(1)
    reduce_four(0)
    for b in range(2):
        r.sums[b, mp] = r.ag_buf[b]
    r.sums[1, 1 - mp] = r.ag_far[1]
    reduce_five(0)
    r.sums[0, 1 - mp] = r.ag_far[0]


def update_kernel(blocks, step, output_src, input_grad_src, sums, *refs):
    params, rest = refs[:15], refs[15:]
    output, input_grad, norm_out = rest[:3]
    targets, news, sem = rest[3:18], rest[18:33], rest[33]
    stores = []

    def store(src, dst):
        copy = pltpu.make_async_copy(src, dst, sem.at[len(stores)])
        copy.start()
        stores.append(copy)

    store(output_src, output)
    store(input_grad_src, input_grad)
    squares = jnp.zeros((8, 128), F32)
    for b in range(2):
        for side in range(2):
            part = sums[b, side].astype(F32)
            squares = squares + fold_rows(part * part)
    squares = jnp.sum(jnp.sum(squares, axis=0, keepdims=True), axis=1, keepdims=True)
    grad_norm = jnp.sqrt(squares)
    norm_out[...] = grad_norm
    clip = jnp.minimum(1.0, CLIP_LIMIT / (grad_norm + 1e-06))
    count = jnp.full((1, 1), step[0], jnp.int32).astype(F32)
    fix_one = 1.0 - jnp.exp2(count * jnp.log2(jnp.full((1, 1), 0.9, F32)))
    fix_two = 1.0 - jnp.exp2(count * jnp.log2(jnp.full((1, 1), 0.999, F32)))
    over_one = 1.0 / fix_one
    over_two = 1.0 / fix_two

    def update(index, where, grad):
        weight, first, second = (params[3 * index + n][where] for n in range(3))
        rate, decay = RATES[index]
        clipped = grad * clip
        first_new = 0.9 * first + 0.1 * clipped
        second_new = 0.999 * second + 0.001 * clipped * clipped
        move = first_new * over_one / (jnp.sqrt(second_new * over_two) + 1e-08)
        if decay:
            move = move + decay * weight
        news[3 * index][where] = weight - rate * move
        news[3 * index + 1][where] = first_new
        news[3 * index + 2][where] = second_new

    lines = {}
    for side in range(2):
        for b in range(2):
            tops = []
            for c in range(blocks):
                block = sums[b, side, pl.ds(c * PART, PART), :].astype(F32)
                update(2 * side, (b, slice(None), slice(c * 128, (c + 1) * 128)), block[0:64])
                tops.append(block[64:72])
            lines[b, side] = jnp.concatenate(tops, axis=1)
        for n in range(3):
            store(news[6 * side + n], targets[6 * side + n])
    for b in range(2):
        update(4, (slice(2 * b, 2 * b + 2), slice(None)), lines[b, 0][0:2])
        update(3, (slice(b, b + 1), slice(None)), lines[b, 1][0:1])
        update(1, (slice(b, b + 1), slice(None)), lines[b, 1][1:2, 0:64])
    for index in (3, 4, 5, 9, 10, 11, 12, 13, 14):
        store(news[index], targets[index])
    for copy in stores:
        copy.wait()


def per_device(
    n_dp,
    tokens,
    lengths,
    cotangent,
    triple_weight,
    query_value_bias,
    output_weight,
    branch_bias,
    expand_weight,
    expand_bias,
    shrink_weight,
    adapter_down,
    down_bias,
    adapter_up,
    up_bias,
    norm_params,
    adapter_down_first,
    adapter_down_second,
    down_bias_first,
    down_bias_second,
    adapter_up_first,
    adapter_up_second,
    up_bias_first,
    up_bias_second,
    norm_params_first,
    norm_params_second,
    step,
):
    tok, width = tokens.shape
    half = triple_weight.shape[2]
    ff_half = expand_weight.shape[1]
    ff = 2 * ff_half
    heads = 2 * half // HEAD_DIM
    blocks = width // 128
    piece = -(-(PART * blocks) // (16 * n_dp)) * 16
    z = types.SimpleNamespace(
        tok=tok,
        width=width,
        half=half,
        ff_half=ff_half,
        ff=ff,
        heads=heads,
        n_dp=n_dp,
        piece=piece,
    )
    flip = lambda v: jnp.swapaxes(v, 1, 2)
    spaces = {
        "s": pl.BlockSpec(memory_space=pltpu.SMEM),
        "v": pl.BlockSpec(memory_space=pltpu.VMEM),
        "h": pl.BlockSpec(memory_space=pltpu.HBM),
    }
    vmem, smem, hbm = spaces["v"], spaces["s"], spaces["h"]
    params = (
        flip(adapter_down),
        flip(adapter_down_first),
        flip(adapter_down_second),
        down_bias,
        down_bias_first,
        down_bias_second,
        adapter_up,
        adapter_up_first,
        adapter_up_second,
        up_bias,
        up_bias_first,
        up_bias_second,
        norm_params,
        norm_params_first,
        norm_params_second,
    )
    operands = (
        lengths,
        query_value_bias,
        branch_bias,
        expand_bias,
        tokens,
        cotangent,
        jnp.transpose(triple_weight, (1, 0, 2)),
        output_weight,
        expand_weight,
        shrink_weight,
        *params,
    )
    output, input_grad, sums, *held = pl.pallas_call(
        functools.partial(layer_kernel, z),
        out_shape=(
            pltpu.VMEM((tok, width), F32),
            pltpu.VMEM((tok, width), F32),
            pltpu.VMEM((2, 2, n_dp, piece, 128), BF),
            *(pltpu.VMEM(p.shape, F32) for p in params),
        ),
        in_specs=[spaces[space] for _, space in INPUTS],
        out_specs=(vmem,) * 18,
        scratch_shapes=[pltpu.VMEM(*make(z)) for _, make in SCRATCH]
        + [
            pltpu.SemaphoreType.DMA((count,)) if count else pltpu.SemaphoreType.REGULAR((2,))
            for _, count in SEMAPHORES
        ]
        + [pltpu.SMEM(lengths.shape, jnp.int32)],
        compiler_params=pltpu.CompilerParams(
            collective_id=0, has_side_effects=True, vmem_limit_bytes=56 * 2**20
        ),
    )(*operands)
    sums = sums.reshape(2, 2, n_dp * piece, 128)
    results = pl.pallas_call(
        functools.partial(update_kernel, blocks),
        out_shape=(
            jax.ShapeDtypeStruct((tok, width), F32),
            jax.ShapeDtypeStruct((tok, width), F32),
            jax.ShapeDtypeStruct((1, 1), F32),
            *(jax.ShapeDtypeStruct(p.shape, F32) for p in params),
        ),
        in_specs=[smem] + [vmem] * 18,
        out_specs=(hbm, hbm, vmem) + (hbm,) * 15,
        scratch_shapes=[pltpu.VMEM(p.shape, F32) for p in params]
        + [pltpu.SemaphoreType.DMA((17,))],
        compiler_params=pltpu.CompilerParams(vmem_limit_bytes=16 * 2**20),
    )(step, output, input_grad, sums, *held)
    news = list(results[3:])
    for index in range(3):
        news[index] = flip(news[index])
    return (results[0], results[1], results[2].reshape(1), *news)


def solution(mesh):
    split = P(("dp", "mp"), None)
    in_specs = (
        split,
        P("dp", None),
        split,
        P(None, None, "mp"),
        P(None, "mp"),
        P("mp", None),
        P(),
        P(None, "mp"),
        P("mp"),
        P("mp", None),
    ) + (P(),) * 16
    out_specs = (split, split) + (P(),) * 16
    return jax.shard_map(
        functools.partial(per_device, mesh.shape["dp"]),
        mesh=mesh,
        in_specs=in_specs,
        out_specs=out_specs,
        check_vma=False,
    )
```
